256 devices in a mesh: dp: 16 (over y, x), row: 4 (over z_hi, core), col: 4 (over z_lo).
Axes of the slice: x: 4, y: 4, z: 8 (z_hi: 2, z_lo: 4; z = z_hi * 4 + z_lo), core: 2. Of those that a mesh axis runs over, the one named last changes fastest.
Arguments:
- tokens: bfloat16 [8192, 3072], P(('dp', 'col'), 'row'), may hold values from -6 to 6
- target: bfloat16 [8192, 3072], P(('dp', 'col'), 'row'), may hold values from -12 to 12
- step_index: int32 [16], P('dp'), may hold values from 0 to 49
- plan: int32 [50], replicated, may hold values from 0 to 999
- w_mod: bfloat16 [256, 9216], replicated, may hold values from -0.375 to 0.375
- w_up: bfloat16 [3072, 6144], P('col', 'row'), may hold values from -0.109375 to 0.109375
- w_down: bfloat16 [6144, 3072], P('col', 'row'), may hold values from -0.078125 to 0.078125
Outputs:
- mean_loss: float32 [], replicated
- grad_up: bfloat16 [3072, 6144], P(('col', 'dp'), 'row')
- grad_down: bfloat16 [6144, 3072], P(('col', 'dp'), 'row')
The draws below stay inside these ranges and needn't reach their ends.
All inputs are finite; a program needn't handle non-finite values.
Results may differ from the reference program's by a relative error of at most 0.017.
Values may be sent and summed in bfloat16 or wider, within the bound.
No kernel may reach another device: no remote copies, remote signals or barrier semaphores. Data moves between devices by JAX's collectives and lax.ppermute only.
A program may use at most 128 MiB of HBM per device.

```python
import math
import jax
import jax.numpy as jnp
from jax import lax

D = 3072
FF = 6144
E = 256
STEPS = 50
TOKENS = 8192
N_DP = 16


def row_scale(low, high):
    place = jnp.arange(TOKENS, dtype=jnp.float32) / max(TOKENS - 1, 1)
    return (low + (high - low) * place)[:, None]


def draw_target(key, part):
    key = jax.random.fold_in(key, 7)
    raw = jnp.clip(jax.random.normal(key, (TOKENS, D), jnp.float32), -4.0, 4.0)
    values = raw * row_scale(0.5, 3.0)
    return values.astype(jnp.bfloat16)


def place_ends(values, stream_key, low, high):
    extent = values.shape
    spot = [jax.random.randint(jax.random.fold_in(stream_key, axis), (), 0, extent[axis]) for axis in range(len(extent))]
    values = values.at[tuple(spot)].set(low)
    longest = extent.index(max(extent))
    spot[longest] = (spot[longest] + 1) % extent[longest]
    return values.at[tuple(spot)].set(high)


def levels(key, shape, split, smallest, top_value):
    loudness, own = 1.0, jax.random.fold_in(key, 6)
    for dim, shards_of in split:
        heights = jnp.exp(jax.random.uniform(jax.random.fold_in(own, dim), (shards_of,), jnp.float32, smallest / len(split), top_value / len(split)))
        loudness = loudness * jnp.repeat(heights, shape[dim] // shards_of).reshape([-1 if axis == dim else 1 for axis in range(len(shape))])
    return loudness


def normal_values(own_key, extent, width, most, shards=(), kind=jnp.bfloat16):
    entries = width * jax.random.normal(own_key, extent, jnp.float32)
    if shards:
        entries = entries * levels(own_key, extent, shards, -0.22, 0.18)
    return jnp.clip(entries, -most, most).astype(kind)


def setup_inputs(seed: int = 0) -> dict:
    streams_of = jax.random.split(jax.random.key(seed), 8)
    tokens = normal_values(streams_of[0], (TOKENS, D), 1.0, 6.0, ((0, 64), (1, 4)))
    target = draw_target(jax.random.fold_in(streams_of[7], 71), 0)
    step_index = place_ends(jax.random.randint(streams_of[2], (N_DP,), 0, STEPS), jax.random.fold_in(streams_of[2], 1), 0, STEPS - 1).astype(jnp.int32)
    plan = place_ends(jax.random.randint(streams_of[3], (STEPS,), 0, 1000), jax.random.fold_in(streams_of[3], 1), 0, 999).astype(jnp.int32)
    w_mod = normal_values(streams_of[4], (E, 3 * D), E ** -0.5, 0.375)
    w_up = normal_values(streams_of[5], (D, FF), D ** -0.5, 0.109375, ((0, 4), (1, 4)))
    w_down = normal_values(streams_of[6], (FF, D), FF ** -0.5, 0.078125, ((0, 4), (1, 4)))
    return dict(tokens=tokens, target=target, step_index=step_index, plan=plan, w_mod=w_mod, w_up=w_up, w_down=w_down)


GELU_COEF = math.sqrt(2.0 / math.pi)
CUBIC_COEF = 0.044715

def gelu_slope(hidden):
    inner = GELU_COEF * (hidden + CUBIC_COEF * hidden * hidden * hidden)
    tanh_value = jnp.tanh(inner)
    return 0.5 * (1.0 + tanh_value) + 0.5 * hidden * (1.0 - tanh_value * tanh_value) * GELU_COEF * (1.0 + 3.0 * CUBIC_COEF * hidden * hidden)

def modulation(step_index, plan, w_mod):
    time_value = plan[step_index].astype(jnp.float32)
    half_width = E // 2
    frequency = jnp.exp(-math.log(10000.0) * jnp.arange(half_width, dtype=jnp.float32) / half_width)
    angles = time_value[:, None] * frequency[None, :]
    embed = jnp.concatenate([jnp.cos(angles), jnp.sin(angles)], axis=1)
    return jnp.dot(jax.nn.silu(embed).astype(jnp.bfloat16), w_mod, preferred_element_type=jnp.float32)

def reference(tokens, target, step_index, plan, w_mod, w_up, w_down):
    mod = modulation(step_index, plan, w_mod)
    group_rows = TOKENS // N_DP
    grad_scale = 1.0 / math.sqrt(TOKENS)
    blocks = tokens.reshape(N_DP, group_rows, D)
    goals = target.reshape(N_DP, group_rows, D)

    def group_step(running, inputs):
        acc_up, acc_down, squares = running
        block, goal, modrow = inputs
        shift = modrow[:D]
        scale = modrow[D:2 * D]
        gate = modrow[2 * D:]
        values = block.astype(jnp.float32)
        average = lax.optimization_barrier(jnp.mean(values, axis=1, keepdims=True))
        centred = values - average
        spread = lax.optimization_barrier(jnp.mean(centred * centred, axis=1, keepdims=True))
        normed = (centred * lax.rsqrt(spread + 1e-06) * (1.0 + scale) + shift).astype(jnp.bfloat16)
        hidden = jnp.dot(normed, w_up, preferred_element_type=jnp.float32)
        activ = jax.nn.gelu(hidden, approximate=True).astype(jnp.bfloat16)
        mixed = jnp.dot(activ, w_down, preferred_element_type=jnp.float32)
        residual = values + gate * mixed - goal.astype(jnp.float32)
        delta_out = (gate * residual * grad_scale).astype(jnp.bfloat16)
        part_down = jnp.dot(activ.T, delta_out, preferred_element_type=jnp.float32)
        hidden_grad = lax.dot_general(delta_out, w_down, (((1,), (1,)), ((), ())), preferred_element_type=jnp.float32)
        delta_hidden = (hidden_grad * gelu_slope(hidden)).astype(jnp.bfloat16)
        part_up = jnp.dot(normed.T, delta_hidden, preferred_element_type=jnp.float32)
        round_up = lax.optimization_barrier(part_up.astype(jnp.bfloat16)).astype(jnp.float32)
        round_down = lax.optimization_barrier(part_down.astype(jnp.bfloat16)).astype(jnp.float32)
        return ((acc_up + round_up, acc_down + round_down, squares + jnp.sum(residual * residual)), None)
    start_state = (jnp.zeros((D, FF), jnp.float32), jnp.zeros((FF, D), jnp.float32), jnp.zeros((), jnp.float32))
    final_state, unused = lax.scan(group_step, start_state, (blocks, goals, mod))
    acc_up, acc_down, squares = final_state
    mean_loss = squares / (TOKENS * D)
    return (mean_loss, acc_up.astype(jnp.bfloat16), acc_down.astype(jnp.bfloat16))
```

```python
import math

import jax
import jax.numpy as jnp
from jax import lax
from jax.sharding import Mesh, PartitionSpec as P

GELU_COEF = math.sqrt(2.0 / math.pi)
CUBIC_COEF = 0.044715
AXES = ("y", "x", "zh", "core", "zl")
SIZES = dict(zip(AXES, (4, 4, 2, 2, 4)))
PLANE = ("y", "x")
DEPTH = ("zh", "zl")
F32 = jnp.float32
BF16 = jnp.bfloat16


def gelu_slope(hidden):
    inner = GELU_COEF * (hidden + CUBIC_COEF * hidden * hidden * hidden)
    tanh_value = jnp.tanh(inner)
    return 0.5 * (1.0 + tanh_value) + 0.5 * hidden * (1.0 - tanh_value * tanh_value) * GELU_COEF * (
        1.0 + 3.0 * CUBIC_COEF * hidden * hidden
    )


def shift_by(value, axis, offset):
    names = (axis,) if isinstance(axis, str) else axis
    count = math.prod(SIZES[name] for name in names)
    return lax.ppermute(value, axis, [(i, (i + offset) % count) for i in range(count)])


def gather_line(value, axis):
    return jnp.stack([value] + [shift_by(value, axis, s) for s in (1, 2, 3)])


def gather_plane(value):
    half = value.shape[0] // 2
    first = gather_line(gather_line(value[:half], "x"), "y")
    second = gather_line(gather_line(value[half:], "y"), "x")
    return jnp.concatenate(
        [first.reshape(16 * half, -1), second.reshape(16 * half, -1)]
    )


def sum_line(blocks, axis):
    parts = [shift_by(blocks[s], axis, -s) for s in (1, 3, 2)]
    return blocks[0].astype(F32) + parts[0].astype(F32) + parts[1].astype(F32) + parts[2].astype(F32)


def sum_plane(value):
    half = value.shape[0] // 2
    grid = value.reshape(2, 4, 4, half // 16, -1)
    first = sum_line(sum_line(grid[0], "y").astype(BF16), "x")
    second = sum_line(sum_line(grid[1], "x").astype(BF16), "y")
    return jnp.concatenate([first, second])


def sum_depth(blocks, place):
    rows = blocks.shape[1] // 2

    def block(offset):
        return lax.dynamic_index_in_dim(blocks, (place + offset) % 8, 0, keepdims=False)

    far = block(4)
    up = shift_by(far[:rows], DEPTH, 1)
    down = shift_by(far[rows:], DEPTH, -1)
    mine = block(3)
    up = jnp.concatenate([(mine[:rows].astype(F32) + up.astype(F32)).astype(BF16), mine[rows:]])
    mine = block(-3)
    down = jnp.concatenate([mine[:rows], (mine[rows:].astype(F32) + down.astype(F32)).astype(BF16)])
    up = shift_by(up, DEPTH, 1)
    down = shift_by(down, DEPTH, -1)
    for offset in (2, 1):
        up = shift_by((block(offset).astype(F32) + up.astype(F32)).astype(BF16), DEPTH, 1)
        down = shift_by((block(-offset).astype(F32) + down.astype(F32)).astype(BF16), DEPTH, -1)
    return (block(0).astype(F32) + up.astype(F32) + down.astype(F32)).astype(BF16)


def dot(a, b, ca, cb):
    return lax.dot_general(a, b, (((ca,), (cb,)), ((), ())), preferred_element_type=F32)


def per_device(tokens, target, step_index, plan, w_mod, w_up, w_down):
    z_half = lax.axis_index("zh")
    core = lax.axis_index("core")
    place = lax.axis_index(DEPTH)
    group = lax.axis_index(PLANE)
    width = tokens.shape[1]
    rows = tokens.shape[0] // 2
    full_width = 4 * width
    token_count = tokens.shape[0] * 64
    piece = w_down.shape[0] // 16

    def by_core(own, other):
        return jnp.where(core == 0, own, other), jnp.where(core == 0, other, own)

    up_part = lax.dynamic_slice_in_dim(w_up, group * piece, piece, 1).T
    down_part = lax.dynamic_slice_in_dim(w_down, group * piece, piece, 0)
    parts = lax.all_gather(jnp.stack([up_part, down_part]), DEPTH, axis=0)
    down = [parts[4 * h : 4 * h + 4, 1].reshape(4 * piece, width) for h in (0, 1)]
    up_all = parts[:, 0].reshape(2, 2, 2, piece, width)
    kept = lax.dynamic_index_in_dim(up_all, core, 2, keepdims=False)
    given = shift_by(lax.dynamic_index_in_dim(up_all, 1 - core, 2, keepdims=False), "core", 1)
    up_pair = by_core(kept, given)
    up = [
        jnp.stack([up_pair[0][:, h], up_pair[1][:, h]], axis=1).reshape(4 * piece, width)
        for h in (0, 1)
    ]

    both = jnp.stack([tokens.reshape(2, rows, width), target.reshape(2, rows, width)], axis=1)
    own = lax.dynamic_index_in_dim(both, z_half, 0, keepdims=False)
    other = shift_by(lax.dynamic_index_in_dim(both, 1 - z_half, 0, keepdims=False), "zh", 1)
    joined = jnp.where(
        z_half == 0, jnp.concatenate([own, other], axis=2), jnp.concatenate([other, own], axis=2)
    ).astype(F32)
    values, goal = joined[0], joined[1]

    picked = jnp.where(jnp.arange(plan.shape[0]) == step_index[0], plan, 0)
    time_value = jnp.sum(picked).astype(F32)
    half_width = w_mod.shape[0] // 2
    frequency = jnp.exp(-math.log(10000.0) * jnp.arange(half_width, dtype=F32) / half_width)
    angles = time_value * frequency
    embed = jnp.concatenate([jnp.cos(angles), jnp.sin(angles)])[None, :]
    mod = jnp.dot(jax.nn.silu(embed).astype(BF16), w_mod, preferred_element_type=F32)
    mod = lax.dynamic_index_in_dim(mod.reshape(3, 2, 2, width), core, 2, keepdims=False)
    shift, scale, gate = mod.reshape(3, 2 * width)

    local_mean = jnp.mean(values, axis=1)
    local_dev = jnp.sum(jnp.square(values - local_mean[:, None]), axis=1)
    far_mean, far_dev = shift_by(jnp.stack([local_mean, local_dev]), "core", 1)
    average = 0.5 * (local_mean + far_mean)
    spread = (
        local_dev + far_dev + jnp.square(local_mean - far_mean) * (0.5 * width * 2)
    ) / full_width
    normed = (
        (values - average[:, None]) * lax.rsqrt(spread + 1e-06)[:, None] * (1.0 + scale) + shift
    ).astype(BF16)

    normed_all = gather_plane(normed)
    hidden = dot(normed_all[:, :width], up[0], 1, 1) + dot(normed_all[:, width:], up[1], 1, 1)
    hidden = hidden + shift_by(hidden, "core", 1)
    activ = jax.nn.gelu(hidden, approximate=True).astype(BF16)
    slope = gelu_slope(hidden)
    mixed = jnp.concatenate([dot(activ, w, 1, 0).astype(BF16) for w in down], axis=1)
    mixed = sum_plane(mixed)
    residual = values + gate * mixed - goal
    squares = jnp.sum(residual * residual)
    for axis in AXES:
        squares = lax.psum(squares, axis)
    mean_loss = squares / (token_count * full_width)
    delta = (gate * residual * (1.0 / math.sqrt(token_count))).astype(BF16)

    delta_all = gather_plane(delta)
    down_blocks = jnp.concatenate(
        [dot(activ, delta_all[:, h * width : (h + 1) * width], 0, 0).astype(BF16) for h in (0, 1)]
    ).reshape(8, piece, width)
    hidden_grad = dot(delta_all[:, :width], down[0], 1, 1) + dot(delta_all[:, width:], down[1], 1, 1)
    hidden_grad = hidden_grad + shift_by(hidden_grad, "core", 1)
    delta_hidden = (hidden_grad * slope).astype(BF16)
    up_grad = jnp.stack(
        [dot(delta_hidden, normed_all[:, h * width : (h + 1) * width], 0, 0).astype(BF16) for h in (0, 1)]
    ).reshape(2, 2, 2, piece, width)
    kept = lax.dynamic_index_in_dim(up_grad, core, 2, keepdims=False)
    given = shift_by(lax.dynamic_index_in_dim(up_grad, 1 - core, 2, keepdims=False), "core", 1)
    pair = by_core(kept, given)
    up_blocks = jnp.stack(pair, axis=2)
    up_blocks = jnp.swapaxes(up_blocks, 0, 1).reshape(8, piece, width)

    grad_down = sum_depth(down_blocks, place)
    grad_up = sum_depth(up_blocks, place)
    grad_up = lax.all_to_all(grad_up.T, PLANE, split_axis=0, concat_axis=1, tiled=True)
    return mean_loss, grad_up, grad_down


def solution(mesh):
    fine = Mesh(mesh.devices.reshape([SIZES[name] for name in AXES]), AXES)
    token_spec = P(("y", "x", "zl"), ("zh", "core"))
    weight_spec = P("zl", ("zh", "core"))
    grad_spec = P(("zl", "y", "x"), ("zh", "core"))
    return jax.shard_map(
        per_device,
        mesh=fine,
        in_specs=(token_spec, token_spec, P(PLANE), P(), P(), weight_spec, weight_spec),
        out_specs=(P(), grad_spec, grad_spec),
        check_vma=False,
    )
```

```python
import math

import jax
import jax.numpy as jnp
from jax import lax
from jax.sharding import Mesh, PartitionSpec as P

GELU_COEF = math.sqrt(2.0 / math.pi)
CUBIC_COEF = 0.044715
AXES = ("y", "x", "zh", "core", "zl")
SIZES = dict(zip(AXES, (4, 4, 2, 2, 4)))
PLANE = ("y", "x")
DEPTH = ("zh", "zl")
F32 = jnp.float32
BF16 = jnp.bfloat16


def gelu_slope(hidden):
    inner = GELU_COEF * (hidden + CUBIC_COEF * hidden * hidden * hidden)
    tanh_value = jnp.tanh(inner)
    return 0.5 * (1.0 + tanh_value) + 0.5 * hidden * (1.0 - tanh_value * tanh_value) * GELU_COEF * (
        1.0 + 3.0 * CUBIC_COEF * hidden * hidden
    )


def shift_by(value, axis, offset):
    names = (axis,) if isinstance(axis, str) else axis
    count = math.prod(SIZES[name] for name in names)
    return lax.ppermute(value, axis, [(i, (i + offset) % count) for i in range(count)])


def turn_by(value, offset, turn):
    ny, nx = SIZES["y"], SIZES["x"]

    def index(y, x, core):
        return ((y % ny) * nx + x % nx) * 2 + core

    pairs = []
    for y in range(ny):
        for x in range(nx):
            for core in range(2):
                along_x = (core == 0) != turn
                goal = index(y, x + offset, core) if along_x else index(y + offset, x, core)
                pairs.append((index(y, x, core), goal))
    return lax.ppermute(value, ("y", "x", "core"), pairs)


def gather_line(value, turn):
    one, three, two = (turn_by(value, s, turn) for s in (1, 3, 2))
    return jnp.stack([value, one, two, three])


def gather_plane(value):
    return gather_line(gather_line(value, False), True)


def sum_line(blocks, turn):
    parts = [turn_by(blocks[s], -s, turn) for s in (1, 3, 2)]
    return blocks[0].astype(F32) + parts[0].astype(F32) + parts[1].astype(F32) + parts[2].astype(F32)


def other_core(value):
    far = shift_by(value, "core", 1)
    return far.reshape(4, 4, -1, far.shape[1]).swapaxes(0, 1).reshape(far.shape)


def sum_everywhere(value):
    value = jnp.full((8, 128), value, F32)
    for axis in AXES:
        size = SIZES[axis]
        for mask in [1, 3][: size.bit_length() - 1]:
            value = value + lax.ppermute(value, axis, [(i, i ^ mask) for i in range(size)])
    return value[0, 0]


def sum_depth(blocks, place):
    rows = blocks.shape[1] // 2

    def block(offset):
        return lax.dynamic_index_in_dim(blocks, (place + offset) % 8, 0, keepdims=False)

    far = block(4)
    up = shift_by(far[:rows], DEPTH, 1)
    down = shift_by(far[rows:], DEPTH, -1)
    mine = block(3)
    up = jnp.concatenate([(mine[:rows].astype(F32) + up.astype(F32)).astype(BF16), mine[rows:]])
    mine = block(-3)
    down = jnp.concatenate([mine[:rows], (mine[rows:].astype(F32) + down.astype(F32)).astype(BF16)])
    up = shift_by(up, DEPTH, 1)
    down = shift_by(down, DEPTH, -1)
    for offset in (2, 1):
        up = shift_by((block(offset).astype(F32) + up.astype(F32)).astype(BF16), DEPTH, 1)
        down = shift_by((block(-offset).astype(F32) + down.astype(F32)).astype(BF16), DEPTH, -1)
    return (block(0).astype(F32) + up.astype(F32) + down.astype(F32)).astype(BF16)


def dot(a, b, ca, cb):
    return lax.dot_general(a, b, (((ca,), (cb,)), ((), ())), preferred_element_type=F32)


def per_device(tokens, target, step_index, plan, w_mod, w_up, w_down):
    z_half = lax.axis_index("zh")
    core = lax.axis_index("core")
    place = lax.axis_index(DEPTH)
    group = lax.axis_index(PLANE)
    width = tokens.shape[1]
    rows = tokens.shape[0] // 2
    full_width = 4 * width
    token_count = tokens.shape[0] * 64
    piece = w_down.shape[0] // 16

    def by_core(own, other):
        return jnp.where(core == 0, own, other), jnp.where(core == 0, other, own)

    up_part = lax.dynamic_slice_in_dim(w_up, group * piece, piece, 1).T
    down_part = lax.dynamic_slice_in_dim(w_down, group * piece, piece, 0)
    parts = lax.all_gather(jnp.stack([up_part, down_part]), DEPTH, axis=0)
    down = jnp.concatenate(
        [parts[4 * h : 4 * h + 4, 1].reshape(4 * piece, width) for h in (0, 1)], axis=1
    )
    up_all = parts[:, 0].reshape(2, 2, 2, piece, width)
    kept = lax.dynamic_index_in_dim(up_all, core, 2, keepdims=False)
    given = shift_by(lax.dynamic_index_in_dim(up_all, 1 - core, 2, keepdims=False), "core", 1)
    up_pair = by_core(kept, given)
    up = jnp.concatenate(
        [
            jnp.stack([up_pair[0][:, h], up_pair[1][:, h]], axis=1).reshape(4 * piece, width)
            for h in (0, 1)
        ],
        axis=1,
    )

    both = jnp.stack([tokens.reshape(2, rows, width), target.reshape(2, rows, width)], axis=1)
    own = lax.dynamic_index_in_dim(both, z_half, 0, keepdims=False)
    other = shift_by(lax.dynamic_index_in_dim(both, 1 - z_half, 0, keepdims=False), "zh", 1)
    joined = jnp.where(
        z_half == 0, jnp.concatenate([own, other], axis=2), jnp.concatenate([other, own], axis=2)
    ).astype(F32)
    values, goal = joined[0], joined[1]

    picked = jnp.where(jnp.arange(plan.shape[0]) == step_index[0], plan, 0)
    time_value = jnp.sum(picked).astype(F32)
    half_width = w_mod.shape[0] // 2
    frequency = jnp.exp(-math.log(10000.0) * jnp.arange(half_width, dtype=F32) / half_width)
    angles = time_value * frequency
    embed = jnp.concatenate([jnp.cos(angles), jnp.sin(angles)])
    level = jax.nn.silu(embed).astype(BF16).astype(F32)
    columns = w_mod.reshape(w_mod.shape[0], 3, 2, 2, width)
    columns = lax.dynamic_index_in_dim(columns, core, 3, keepdims=False)
    mod = jnp.sum(level[:, None, None, None] * columns.astype(F32), axis=0)
    shift, scale, gate = mod.reshape(3, 2 * width)

    local_mean = jnp.mean(values, axis=1)
    local_dev = jnp.sum(jnp.square(values - local_mean[:, None]), axis=1)
    far_mean, far_dev = shift_by(jnp.stack([local_mean, local_dev]), "core", 1)
    average = 0.5 * (local_mean + far_mean)
    spread = (
        local_dev + far_dev + jnp.square(local_mean - far_mean) * (0.5 * width * 2)
    ) / full_width
    normed = (
        (values - average[:, None]) * lax.rsqrt(spread + 1e-06)[:, None] * (1.0 + scale) + shift
    ).astype(BF16)

    normed_all = gather_plane(normed).reshape(16 * rows, 2 * width)
    hidden = dot(normed_all, up, 1, 1)
    hidden = hidden + other_core(hidden)
    activ = jax.nn.gelu(hidden, approximate=True).astype(BF16)
    slope = gelu_slope(hidden)
    line = activ.reshape(4, 4 * rows, 4 * piece)
    mixed = {s: dot(line[s], down, 1, 0).astype(BF16) for s in (1, 3, 2, 0)}
    mixed = sum_line(mixed, True).astype(BF16)
    mixed = sum_line(mixed.reshape(4, rows, 2 * width), False)
    residual = values + gate * mixed - goal
    squares = sum_everywhere(jnp.sum(residual * residual))
    mean_loss = squares / (token_count * full_width)
    delta = (gate * residual * (1.0 / math.sqrt(token_count))).astype(BF16)

    delta_all = gather_plane(delta).reshape(16 * rows, 2 * width)
    hidden_grad = dot(delta_all, down, 1, 1)
    hidden_grad = hidden_grad + other_core(hidden_grad)
    down_blocks = jnp.concatenate(
        [dot(activ, delta_all[:, h * width : (h + 1) * width], 0, 0).astype(BF16) for h in (0, 1)]
    ).reshape(8, piece, width)
    delta_hidden = (hidden_grad * slope).astype(BF16)
    up_grad = jnp.stack(
        [dot(delta_hidden, normed_all[:, h * width : (h + 1) * width], 0, 0).astype(BF16) for h in (0, 1)]
    ).reshape(2, 2, 2, piece, width)
    kept = lax.dynamic_index_in_dim(up_grad, core, 2, keepdims=False)
    given = shift_by(lax.dynamic_index_in_dim(up_grad, 1 - core, 2, keepdims=False), "core", 1)
    pair = by_core(kept, given)
    up_blocks = jnp.stack(pair, axis=2)
    up_blocks = jnp.swapaxes(up_blocks, 0, 1).reshape(8, piece, width)

    grad_down = sum_depth(down_blocks, place)
    grad_up = sum_depth(up_blocks, place)
    grad_up = lax.all_to_all(grad_up.T, PLANE, split_axis=0, concat_axis=1, tiled=True)
    return mean_loss, grad_up, grad_down


def solution(mesh):
    fine = Mesh(mesh.devices.reshape([SIZES[name] for name in AXES]), AXES)
    token_spec = P(("y", "x", "zl"), ("zh", "core"))
    weight_spec = P("zl", ("zh", "core"))
    grad_spec = P(("zl", "y", "x"), ("zh", "core"))
    return jax.shard_map(
        per_device,
        mesh=fine,
        in_specs=(token_spec, token_spec, P(PLANE), P(), P(), weight_spec, weight_spec),
        out_specs=(P(), grad_spec, grad_spec),
        check_vma=False,
    )
```

```python
import math

import jax
import jax.numpy as jnp
from jax import lax
from jax.experimental import pallas as pl
from jax.experimental.pallas import tpu as pltpu
from jax.sharding import Mesh, PartitionSpec as P

GELU_COEF = math.sqrt(2.0 / math.pi)
CUBIC_COEF = 0.044715
AXES = ("y", "x", "zh", "core", "zl")
SIZES = dict(zip(AXES, (4, 4, 2, 2, 4)))
PLANE = ("y", "x")
DEPTH = ("zh", "zl")
F32 = jnp.float32
BF16 = jnp.bfloat16


def gelu_slope(hidden):
    inner = GELU_COEF * (hidden + CUBIC_COEF * hidden * hidden * hidden)
    tanh_value = jnp.tanh(inner)
    return 0.5 * (1.0 + tanh_value) + 0.5 * hidden * (1.0 - tanh_value * tanh_value) * GELU_COEF * (
        1.0 + 3.0 * CUBIC_COEF * hidden * hidden
    )


def shift_by(value, axis, offset):
    names = (axis,) if isinstance(axis, str) else axis
    count = math.prod(SIZES[name] for name in names)
    return lax.ppermute(value, axis, [(i, (i + offset) % count) for i in range(count)])


def turn_by(value, offset, turn):
    ny, nx = SIZES["y"], SIZES["x"]

    def index(y, x, core):
        return ((y % ny) * nx + x % nx) * 2 + core

    pairs = []
    for y in range(ny):
        for x in range(nx):
            for core in range(2):
                along_x = (core == 0) != turn
                goal = index(y, x + offset, core) if along_x else index(y + offset, x, core)
                pairs.append((index(y, x, core), goal))
    return lax.ppermute(value, ("y", "x", "core"), pairs)


def gather_line(value, turn):
    one, three, two = (turn_by(value, s, turn) for s in (1, 3, 2))
    return jnp.stack([value, one, two, three])


def gather_plane(value):
    return gather_line(gather_line(value, False), True)


def sum_line(blocks, turn):
    parts = [turn_by(blocks[s], -s, turn) for s in (1, 3, 2)]
    return blocks[0].astype(F32) + parts[0].astype(F32) + parts[1].astype(F32) + parts[2].astype(F32)


def other_core(value):
    far = shift_by(value, "core", 1)
    return far.reshape(4, 4, -1, far.shape[1]).swapaxes(0, 1).reshape(far.shape)


def as_triple(value):
    high = lax.reduce_precision(value, 8, 7)
    middle = lax.reduce_precision(value - high, 8, 7)
    return jnp.stack([high, middle, value - high - middle])


def modulate(level, w_mod, core):
    width = w_mod.shape[1] // 12
    depth = w_mod.shape[0]

    def body(core_ref, level_ref, w_ref, out_ref):
        out_ref[...] = jnp.dot(level_ref[...], w_ref[...], preferred_element_type=F32)

    return pl.pallas_call(
        body,
        grid_spec=pltpu.PrefetchScalarGridSpec(
            num_scalar_prefetch=1,
            grid=(6,),
            in_specs=[
                pl.BlockSpec((16, depth), lambda j, core_ref: (0, 0)),
                pl.BlockSpec(
                    (depth, width), lambda j, core_ref: (0, (j // 2) * 4 + (j % 2) * 2 + core_ref[0])
                ),
            ],
            out_specs=pl.BlockSpec((16, width), lambda j, core_ref: (0, j)),
        ),
        out_shape=jax.ShapeDtypeStruct((16, 6 * width), F32),
        cost_estimate=pl.CostEstimate(
            flops=2 * 16 * depth * 6 * width, bytes_accessed=2 * depth * 6 * width, transcendentals=0
        ),
        name="modulate",
    )(core.reshape(1).astype(jnp.int32), jnp.broadcast_to(level, (16, depth)), w_mod)[0]


def sum_depth(blocks, place, extra=None):
    half = blocks.shape[1] // 2
    tail = [] if extra is None else [extra]

    def block(offset):
        own = lax.dynamic_index_in_dim(blocks, (place + offset) % 8, 0, keepdims=False)
        return jnp.concatenate([own] + tail)

    def add(a, b):
        return (a.astype(F32) + b.astype(F32)).astype(BF16)

    far = block(4)
    up = shift_by(far[:half], DEPTH, 1)
    down = shift_by(far[half:], DEPTH, -1)
    mine = block(3)
    up = jnp.concatenate([add(mine[:half], up), mine[half:]])
    mine = block(-3)
    down = jnp.concatenate([mine[:half], add(mine[half:], down)])
    up = shift_by(up, DEPTH, 1)
    down = shift_by(down, DEPTH, -1)
    for offset in (2, 1):
        up = shift_by(add(block(offset), up), DEPTH, 1)
        down = shift_by(add(block(-offset), down), DEPTH, -1)
    return (block(0).astype(F32) + up.astype(F32) + down.astype(F32)).astype(BF16)


def dot(a, b, ca, cb):
    return lax.dot_general(a, b, (((ca,), (cb,)), ((), ())), preferred_element_type=F32)


def per_device(tokens, target, step_index, plan, w_mod, w_up, w_down):
    z_half = lax.axis_index("zh")
    core = lax.axis_index("core")
    place = lax.axis_index(DEPTH)
    group = lax.axis_index(PLANE)
    width = tokens.shape[1]
    rows = tokens.shape[0] // 2
    full_width = 4 * width
    token_count = tokens.shape[0] * 64
    piece = w_down.shape[0] // 16

    def by_core(own, other):
        return jnp.where(core == 0, own, other), jnp.where(core == 0, other, own)

    up_part = lax.dynamic_slice_in_dim(w_up, group * piece, piece, 1).T
    down_part = lax.dynamic_slice_in_dim(w_down, group * piece, piece, 0)
    parts = lax.all_gather(jnp.stack([up_part, down_part]), DEPTH, axis=0)
    down = jnp.concatenate(
        [parts[4 * h : 4 * h + 4, 1].reshape(4 * piece, width) for h in (0, 1)], axis=1
    )
    up_all = parts[:, 0].reshape(2, 2, 2, piece, width)
    kept = lax.dynamic_index_in_dim(up_all, core, 2, keepdims=False)
    given = shift_by(lax.dynamic_index_in_dim(up_all, 1 - core, 2, keepdims=False), "core", 1)
    up_pair = by_core(kept, given)
    up = jnp.concatenate(
        [
            jnp.stack([up_pair[0][:, h], up_pair[1][:, h]], axis=1).reshape(4 * piece, width)
            for h in (0, 1)
        ],
        axis=1,
    )

    both = jnp.stack([tokens.reshape(2, rows, width), target.reshape(2, rows, width)], axis=1)
    own = lax.dynamic_index_in_dim(both, z_half, 0, keepdims=False)
    other = shift_by(lax.dynamic_index_in_dim(both, 1 - z_half, 0, keepdims=False), "zh", 1)
    joined = jnp.where(
        z_half == 0, jnp.concatenate([own, other], axis=2), jnp.concatenate([other, own], axis=2)
    ).astype(F32)
    values, goal = joined[0], joined[1]

    picked = jnp.where(jnp.arange(plan.shape[0]) == step_index[0], plan, 0)
    time_value = jnp.sum(picked).astype(F32)
    half_width = w_mod.shape[0] // 2
    frequency = jnp.exp(-math.log(10000.0) * jnp.arange(half_width, dtype=F32) / half_width)
    angles = time_value * frequency
    embed = jnp.concatenate([jnp.cos(angles), jnp.sin(angles)])
    mod = modulate(jax.nn.silu(embed).astype(BF16), w_mod, core)
    shift, scale, gate = mod.reshape(3, 2 * width)

    local_mean = jnp.mean(values, axis=1)
    local_dev = jnp.sum(jnp.square(values - local_mean[:, None]), axis=1)
    far_mean, far_dev = shift_by(jnp.stack([local_mean, local_dev]), "core", 1)
    average = 0.5 * (local_mean + far_mean)
    spread = (
        local_dev + far_dev + jnp.square(local_mean - far_mean) * (0.5 * width * 2)
    ) / full_width
    normed = (
        (values - average[:, None]) * lax.rsqrt(spread + 1e-06)[:, None] * (1.0 + scale) + shift
    ).astype(BF16)

    normed_all = gather_plane(normed).reshape(16 * rows, 2 * width)
    hidden = dot(normed_all, up, 1, 1)
    hidden = hidden + other_core(hidden)
    activ = jax.nn.gelu(hidden, approximate=True).astype(BF16)
    slope = gelu_slope(hidden)
    line = activ.reshape(4, 4 * rows, 4 * piece)
    mixed = {s: dot(line[s], down, 1, 0).astype(BF16) for s in (1, 3, 2, 0)}
    mixed = sum_line(mixed, True).astype(BF16)
    mixed = sum_line(mixed.reshape(4, rows, 2 * width), False)
    residual = values + gate * mixed - goal
    squares = jnp.full((8, 128), jnp.sum(residual * residual), F32)
    squares = (squares + shift_by(squares, "core", 1))[0, 0]
    delta = (gate * residual * (1.0 / math.sqrt(token_count))).astype(BF16)

    delta_all = gather_plane(delta).reshape(16 * rows, 2 * width)
    hidden_grad = dot(delta_all, down, 1, 1)
    hidden_grad = hidden_grad + other_core(hidden_grad)
    down_blocks = jnp.concatenate(
        [dot(activ, delta_all[:, h * width : (h + 1) * width], 0, 0).astype(BF16) for h in (0, 1)]
    ).reshape(8, piece, width)
    delta_hidden = (hidden_grad * slope).astype(BF16)
    up_grad = jnp.stack(
        [dot(delta_hidden, normed_all[:, h * width : (h + 1) * width], 0, 0).astype(BF16) for h in (0, 1)]
    ).reshape(2, 2, 2, piece, width)
    kept = lax.dynamic_index_in_dim(up_grad, core, 2, keepdims=False)
    given = shift_by(lax.dynamic_index_in_dim(up_grad, 1 - core, 2, keepdims=False), "core", 1)
    pair = by_core(kept, given)
    up_blocks = jnp.stack(pair, axis=2)
    up_blocks = jnp.swapaxes(up_blocks, 0, 1).reshape(8, piece, width)

    terms = as_triple(squares)
    slots = jnp.where(jnp.arange(8)[:, None] == place, terms[None, :], 0.0).reshape(24)
    extra = jnp.zeros((16, width), BF16).at[0, :24].set(slots.astype(BF16))
    grad_down = sum_depth(down_blocks, place, extra)
    terms = as_triple(jnp.sum(grad_down[piece, :24].astype(F32)))
    grad_down = grad_down[:piece]
    grad_up = sum_depth(up_blocks, place).T.reshape(16, -1, piece)
    share = grad_up.shape[1]
    note = jnp.zeros((16, 16, piece), BF16).at[:, 0, :3].set(terms.astype(BF16))
    grad_up = lax.all_to_all(
        jnp.concatenate([grad_up, note], axis=1), PLANE, split_axis=0, concat_axis=0, tiled=True
    )
    squares = jnp.sum(grad_up[:, share, :3].astype(F32))
    mean_loss = squares / (token_count * full_width)
    grad_up = jnp.swapaxes(grad_up[:, :share], 0, 1).reshape(share, -1)
    return mean_loss, grad_up, grad_down


def solution(mesh):
    fine = Mesh(mesh.devices.reshape([SIZES[name] for name in AXES]), AXES)
    token_spec = P(("y", "x", "zl"), ("zh", "core"))
    weight_spec = P("zl", ("zh", "core"))
    grad_spec = P(("zl", "y", "x"), ("zh", "core"))
    return jax.shard_map(
        per_device,
        mesh=fine,
        in_specs=(token_spec, token_spec, P(PLANE), P(), P(), weight_spec, weight_spec),
        out_specs=(P(), grad_spec, grad_spec),
        check_vma=False,
    )
```

```python
import math

import jax
import jax.numpy as jnp
from jax import lax
from jax.experimental import pallas as pl
from jax.experimental.pallas import tpu as pltpu
from jax.sharding import Mesh, PartitionSpec as P

GELU_COEF = math.sqrt(2.0 / math.pi)
CUBIC_COEF = 0.044715
AXES = ("y", "x", "zh", "core", "zl")
SIZES = dict(zip(AXES, (4, 4, 2, 2, 4)))
PLANE = ("y", "x")
DEPTH = ("zh", "zl")
F32 = jnp.float32
BF16 = jnp.bfloat16


def gelu_slope(hidden):
    inner = GELU_COEF * (hidden + CUBIC_COEF * hidden * hidden * hidden)
    tanh_value = jnp.tanh(inner)
    return 0.5 * (1.0 + tanh_value) + 0.5 * hidden * (1.0 - tanh_value * tanh_value) * GELU_COEF * (
        1.0 + 3.0 * CUBIC_COEF * hidden * hidden
    )


def shift_by(value, axis, offset):
    names = (axis,) if isinstance(axis, str) else axis
    count = math.prod(SIZES[name] for name in names)
    return lax.ppermute(value, axis, [(i, (i + offset) % count) for i in range(count)])


def turn_by(value, offset, turn):
    ny, nx = SIZES["y"], SIZES["x"]

    def index(y, x, core):
        return ((y % ny) * nx + x % nx) * 2 + core

    pairs = []
    for y in range(ny):
        for x in range(nx):
            for core in range(2):
                along_x = (core == 0) != turn
                goal = index(y, x + offset, core) if along_x else index(y + offset, x, core)
                pairs.append((index(y, x, core), goal))
    return lax.ppermute(value, ("y", "x", "core"), pairs)


def gather_line(value, turn):
    one, three, two = (turn_by(value, s, turn) for s in (1, 3, 2))
    return jnp.stack([value, one, two, three])


def gather_plane(value):
    return gather_line(gather_line(value, False), True)


def sum_line(blocks, turn):
    parts = [turn_by(blocks[s], -s, turn) for s in (1, 3, 2)]
    return blocks[0].astype(F32) + parts[0].astype(F32) + parts[1].astype(F32) + parts[2].astype(F32)


def other_core(value):
    far = shift_by(value, "core", 1)
    return far.reshape(4, 4, -1, far.shape[1]).swapaxes(0, 1).reshape(far.shape)


def as_triple(value):
    high = lax.reduce_precision(value, 8, 7)
    middle = lax.reduce_precision(value - high, 8, 7)
    return jnp.stack([high, middle, value - high - middle])


def modulate(level, w_mod, core):
    width = w_mod.shape[1] // 12
    depth = w_mod.shape[0]

    def body(core_ref, level_ref, w_ref, out_ref):
        out_ref[...] = jnp.dot(level_ref[...], w_ref[...], preferred_element_type=F32)

    return pl.pallas_call(
        body,
        grid_spec=pltpu.PrefetchScalarGridSpec(
            num_scalar_prefetch=1,
            grid=(6,),
            in_specs=[
                pl.BlockSpec((16, depth), lambda j, core_ref: (0, 0)),
                pl.BlockSpec(
                    (depth, width), lambda j, core_ref: (0, (j // 2) * 4 + (j % 2) * 2 + core_ref[0])
                ),
            ],
            out_specs=pl.BlockSpec((16, width), lambda j, core_ref: (0, j)),
        ),
        out_shape=jax.ShapeDtypeStruct((16, 6 * width), F32),
        cost_estimate=pl.CostEstimate(
            flops=2 * 16 * depth * 6 * width, bytes_accessed=2 * depth * 6 * width, transcendentals=0
        ),
        name="modulate",
    )(core.reshape(1).astype(jnp.int32), jnp.broadcast_to(level, (16, depth)), w_mod)[0]


def sum_depth(blocks, place):
    half = blocks.shape[1] // 2

    def block(offset):
        return lax.dynamic_index_in_dim(blocks, (place + offset) % 8, 0, keepdims=False)

    def add(a, b):
        return (a.astype(F32) + b.astype(F32)).astype(BF16)

    far = block(4)
    up = shift_by(far[:half], DEPTH, 1)
    down = shift_by(far[half:], DEPTH, -1)
    mine = block(3)
    up = jnp.concatenate([add(mine[:half], up), mine[half:]])
    mine = block(-3)
    down = jnp.concatenate([mine[:half], add(mine[half:], down)])
    up = shift_by(up, DEPTH, 1)
    down = shift_by(down, DEPTH, -1)
    for offset in (2, 1):
        up = shift_by(add(block(offset), up), DEPTH, 1)
        down = shift_by(add(block(-offset), down), DEPTH, -1)
    return (block(0).astype(F32) + up.astype(F32) + down.astype(F32)).astype(BF16)


def dot(a, b, ca, cb):
    return lax.dot_general(a, b, (((ca,), (cb,)), ((), ())), preferred_element_type=F32)


def per_device(tokens, target, step_index, plan, w_mod, w_up, w_down):
    z_half = lax.axis_index("zh")
    core = lax.axis_index("core")
    place = lax.axis_index(DEPTH)
    group = lax.axis_index(PLANE)
    width = tokens.shape[1]
    rows = tokens.shape[0] // 2
    full_width = 4 * width
    token_count = tokens.shape[0] * 64
    piece = w_down.shape[0] // 16

    def by_core(own, other):
        return jnp.where(core == 0, own, other), jnp.where(core == 0, other, own)

    up_part = lax.dynamic_slice_in_dim(w_up, group * piece, piece, 1).T
    down_part = lax.dynamic_slice_in_dim(w_down, group * piece, piece, 0)
    parts = lax.all_gather(jnp.stack([up_part, down_part]), DEPTH, axis=0)
    down = jnp.concatenate(
        [parts[4 * h : 4 * h + 4, 1].reshape(4 * piece, width) for h in (0, 1)], axis=1
    )
    up_all = parts[:, 0].reshape(2, 2, 2, piece, width)
    kept = lax.dynamic_index_in_dim(up_all, core, 2, keepdims=False)
    given = shift_by(lax.dynamic_index_in_dim(up_all, 1 - core, 2, keepdims=False), "core", 1)
    up_pair = by_core(kept, given)
    up = jnp.concatenate(
        [
            jnp.stack([up_pair[0][:, h], up_pair[1][:, h]], axis=1).reshape(4 * piece, width)
            for h in (0, 1)
        ],
        axis=1,
    )

    both = jnp.stack([tokens.reshape(2, rows, width), target.reshape(2, rows, width)], axis=1)
    own = lax.dynamic_index_in_dim(both, z_half, 0, keepdims=False)
    other = shift_by(lax.dynamic_index_in_dim(both, 1 - z_half, 0, keepdims=False), "zh", 1)
    joined = jnp.where(
        z_half == 0, jnp.concatenate([own, other], axis=2), jnp.concatenate([other, own], axis=2)
    ).astype(F32)
    values, goal = joined[0], joined[1]

    picked = jnp.where(jnp.arange(plan.shape[0]) == step_index[0], plan, 0)
    time_value = jnp.sum(picked).astype(F32)
    half_width = w_mod.shape[0] // 2
    frequency = jnp.exp(-math.log(10000.0) * jnp.arange(half_width, dtype=F32) / half_width)
    angles = time_value * frequency
    embed = jnp.concatenate([jnp.cos(angles), jnp.sin(angles)])
    mod = modulate(jax.nn.silu(embed).astype(BF16), w_mod, core)
    shift, scale, gate = mod.reshape(3, 2 * width)

    local_mean = jnp.mean(values, axis=1)
    local_dev = jnp.sum(jnp.square(values - local_mean[:, None]), axis=1)
    far_mean, far_dev = shift_by(jnp.stack([local_mean, local_dev]), "core", 1)
    average = 0.5 * (local_mean + far_mean)
    spread = (
        local_dev + far_dev + jnp.square(local_mean - far_mean) * (0.5 * width * 2)
    ) / full_width
    normed = (
        (values - average[:, None]) * lax.rsqrt(spread + 1e-06)[:, None] * (1.0 + scale) + shift
    ).astype(BF16)

    normed_all = gather_plane(normed).reshape(16 * rows, 2 * width)
    hidden = dot(normed_all, up, 1, 1)
    hidden = hidden + other_core(hidden)
    activ = jax.nn.gelu(hidden, approximate=True).astype(BF16)
    activ, slope = lax.optimization_barrier((activ, gelu_slope(hidden)))
    line = activ.reshape(4, 4 * rows, 4 * piece)
    mixed = {s: dot(line[s], down, 1, 0).astype(BF16) for s in (1, 3, 2, 0)}
    mixed = sum_line(mixed, True).astype(BF16)
    mixed = sum_line(mixed.reshape(4, rows, 2 * width), False)
    residual = values + gate * mixed - goal
    squares = jnp.full((8, 128), jnp.sum(residual * residual), F32)
    squares = (squares + shift_by(squares, "core", 1))[0, 0]
    delta = (gate * residual * (1.0 / math.sqrt(token_count))).astype(BF16)

    delta_all = gather_plane(delta).reshape(16 * rows, 2 * width)
    hidden_grad = dot(delta_all, down, 1, 1)
    hidden_grad = hidden_grad + other_core(hidden_grad)
    down_blocks = jnp.concatenate(
        [dot(activ, delta_all[:, h * width : (h + 1) * width], 0, 0).astype(BF16) for h in (0, 1)]
    ).reshape(8, piece, width)
    delta_hidden = (hidden_grad * slope).astype(BF16)
    up_grad = jnp.stack(
        [dot(delta_hidden, normed_all[:, h * width : (h + 1) * width], 0, 0).astype(BF16) for h in (0, 1)]
    ).reshape(2, 2, 2, piece, width)
    kept = lax.dynamic_index_in_dim(up_grad, core, 2, keepdims=False)
    given = shift_by(lax.dynamic_index_in_dim(up_grad, 1 - core, 2, keepdims=False), "core", 1)
    pair = by_core(kept, given)
    up_blocks = jnp.stack(pair, axis=2)
    up_blocks = jnp.swapaxes(up_blocks, 0, 1).reshape(8, piece, width)

    terms = as_triple(squares)
    slots = jnp.where(jnp.arange(8)[:, None] == place, terms[None, :], 0.0).reshape(24)
    extra = jnp.zeros((16, width), BF16).at[0, :24].set(slots.astype(BF16))
    extra = jnp.broadcast_to(extra, (8, 16, width))
    grad_down = jnp.concatenate([down_blocks, extra], axis=1).reshape(-1, width)
    grad_down = lax.psum_scatter(grad_down, DEPTH, scatter_dimension=0, tiled=True)
    terms = as_triple(jnp.sum(grad_down[piece, :24].astype(F32)))
    grad_down = grad_down[:piece]
    grad_up = sum_depth(up_blocks, place).T.reshape(16, -1, piece)
    share = grad_up.shape[1]
    note = jnp.zeros((16, 16, piece), BF16).at[:, 0, :3].set(terms.astype(BF16))
    grad_up = lax.all_to_all(
        jnp.concatenate([grad_up, note], axis=1), PLANE, split_axis=0, concat_axis=0, tiled=True
    )
    squares = jnp.sum(grad_up[:, share, :3].astype(F32))
    mean_loss = squares / (token_count * full_width)
    grad_up = jnp.swapaxes(grad_up[:, :share], 0, 1).reshape(share, -1)
    return mean_loss, grad_up, grad_down


def solution(mesh):
    fine = Mesh(mesh.devices.reshape([SIZES[name] for name in AXES]), AXES)
    token_spec = P(("y", "x", "zl"), ("zh", "core"))
    weight_spec = P("zl", ("zh", "core"))
    grad_spec = P(("zl", "y", "x"), ("zh", "core"))
    return jax.shard_map(
        per_device,
        mesh=fine,
        in_specs=(token_spec, token_spec, P(PLANE), P(), P(), weight_spec, weight_spec),
        out_specs=(P(), grad_spec, grad_spec),
        check_vma=False,
    )
```

```python
import math

import jax
import jax.numpy as jnp
from jax import lax
from jax.experimental import pallas as pl
from jax.experimental.pallas import tpu as pltpu
from jax.sharding import Mesh, PartitionSpec as P

GELU_COEF = math.sqrt(2.0 / math.pi)
CUBIC_COEF = 0.044715
AXES = ("y", "x", "zh", "core", "zl")
SIZES = dict(zip(AXES, (4, 4, 2, 2, 4)))
PLANE = ("y", "x")
DEPTH = ("zh", "zl")
F32 = jnp.float32
BF16 = jnp.bfloat16


def gelu_slope(hidden):
    inner = GELU_COEF * (hidden + CUBIC_COEF * hidden * hidden * hidden)
    tanh_value = jnp.tanh(inner)
    return 0.5 * (1.0 + tanh_value) + 0.5 * hidden * (1.0 - tanh_value * tanh_value) * GELU_COEF * (
        1.0 + 3.0 * CUBIC_COEF * hidden * hidden
    )


def shift_by(value, axis, offset):
    names = (axis,) if isinstance(axis, str) else axis
    count = math.prod(SIZES[name] for name in names)
    return lax.ppermute(value, axis, [(i, (i + offset) % count) for i in range(count)])


def turn_by(value, offset, turn):
    ny, nx = SIZES["y"], SIZES["x"]

    def index(y, x, core):
        return ((y % ny) * nx + x % nx) * 2 + core

    pairs = []
    for y in range(ny):
        for x in range(nx):
            for core in range(2):
                along_x = (core == 0) != turn
                goal = index(y, x + offset, core) if along_x else index(y + offset, x, core)
                pairs.append((index(y, x, core), goal))
    return lax.ppermute(value, ("y", "x", "core"), pairs)


def gather_line(value, turn):
    one, three, two = (turn_by(value, s, turn) for s in (1, 3, 2))
    return jnp.stack([value, one, two, three])


def gather_plane(value):
    return gather_line(gather_line(value, False), True)


def sum_line(blocks, turn):
    parts = [turn_by(blocks[s], -s, turn) for s in (1, 3, 2)]
    return blocks[0].astype(F32) + parts[0].astype(F32) + parts[1].astype(F32) + parts[2].astype(F32)


def other_core(value):
    far = shift_by(value, "core", 1)
    return far.reshape(4, 4, -1, far.shape[1]).swapaxes(0, 1).reshape(far.shape)


def as_triple(value, first, shape):
    value = jnp.broadcast_to(value, shape)
    lane = lax.broadcasted_iota(jnp.int32, shape, len(shape) - 1) - first
    high = lax.reduce_precision(value, 8, 7)
    middle = lax.reduce_precision(value - high, 8, 7)
    low = value - high - middle
    terms = jnp.where(lane == 0, high, jnp.where(lane == 1, middle, low))
    return jnp.where((lane >= 0) & (lane < 3), terms, 0.0).astype(BF16)


def modulate(level, w_mod, core):
    width = w_mod.shape[1] // 12
    depth = w_mod.shape[0]

    def body(core_ref, level_ref, w_ref, out_ref):
        out_ref[...] = jnp.dot(level_ref[...], w_ref[...], preferred_element_type=F32)

    return pl.pallas_call(
        body,
        grid_spec=pltpu.PrefetchScalarGridSpec(
            num_scalar_prefetch=1,
            grid=(6,),
            in_specs=[
                pl.BlockSpec((16, depth), lambda j, core_ref: (0, 0)),
                pl.BlockSpec(
                    (depth, width), lambda j, core_ref: (0, (j // 2) * 4 + (j % 2) * 2 + core_ref[0])
                ),
            ],
            out_specs=pl.BlockSpec((16, width), lambda j, core_ref: (0, j)),
        ),
        out_shape=jax.ShapeDtypeStruct((16, 6 * width), F32),
        cost_estimate=pl.CostEstimate(
            flops=2 * 16 * depth * 6 * width, bytes_accessed=2 * depth * 6 * width, transcendentals=0
        ),
        name="modulate",
    )(core.reshape(1).astype(jnp.int32), jnp.broadcast_to(level, (16, depth)), w_mod)[0]


def sum_depth(blocks, place):
    half = blocks.shape[1] // 2

    def block(offset):
        return lax.dynamic_index_in_dim(
            blocks, jnp.bitwise_and(place + offset, 7).astype(jnp.uint32), 0, keepdims=False
        )

    def add(a, b):
        return (a.astype(F32) + b.astype(F32)).astype(BF16)

    far = block(4)
    up = shift_by(far[:half], DEPTH, 1)
    down = shift_by(far[half:], DEPTH, -1)
    mine = block(3)
    up = jnp.concatenate([add(mine[:half], up), mine[half:]])
    mine = block(-3)
    down = jnp.concatenate([mine[:half], add(mine[half:], down)])
    up = shift_by(up, DEPTH, 1)
    down = shift_by(down, DEPTH, -1)
    for offset in (2, 1):
        up = shift_by(add(block(offset), up), DEPTH, 1)
        down = shift_by(add(block(-offset), down), DEPTH, -1)
    return (block(0).astype(F32) + up.astype(F32) + down.astype(F32)).astype(BF16)


def dot(a, b, ca, cb):
    return lax.dot_general(a, b, (((ca,), (cb,)), ((), ())), preferred_element_type=F32)


def per_device(tokens, target, step_index, plan, w_mod, w_up, w_down):
    z_half = lax.axis_index("zh")
    core = lax.axis_index("core")
    place = lax.axis_index(DEPTH)
    group = lax.axis_index(PLANE)
    width = tokens.shape[1]
    rows = tokens.shape[0] // 2
    full_width = 4 * width
    token_count = tokens.shape[0] * 64
    piece = w_down.shape[0] // 16

    def by_core(own, other):
        return jnp.where(core == 0, own, other), jnp.where(core == 0, other, own)

    up_part = lax.dynamic_slice_in_dim(w_up, group * piece, piece, 1).T
    down_part = lax.dynamic_slice_in_dim(w_down, group * piece, piece, 0)
    parts = lax.all_gather(jnp.stack([up_part, down_part]), DEPTH, axis=0)
    down = jnp.concatenate(
        [parts[4 * h : 4 * h + 4, 1].reshape(4 * piece, width) for h in (0, 1)], axis=1
    )
    up_all = parts[:, 0].reshape(2, 2, 2, piece, width)
    kept = lax.dynamic_index_in_dim(up_all, core, 2, keepdims=False)
    given = shift_by(lax.dynamic_index_in_dim(up_all, 1 - core, 2, keepdims=False), "core", 1)
    up_pair = by_core(kept, given)
    up = jnp.concatenate(
        [
            jnp.stack([up_pair[0][:, h], up_pair[1][:, h]], axis=1).reshape(4 * piece, width)
            for h in (0, 1)
        ],
        axis=1,
    )

    both = jnp.stack([tokens.reshape(2, rows, width), target.reshape(2, rows, width)], axis=1)
    own = lax.dynamic_index_in_dim(both, z_half, 0, keepdims=False)
    other = shift_by(lax.dynamic_index_in_dim(both, 1 - z_half, 0, keepdims=False), "zh", 1)
    joined = jnp.where(
        z_half == 0, jnp.concatenate([own, other], axis=2), jnp.concatenate([other, own], axis=2)
    ).astype(F32)
    values, goal = joined[0], joined[1]

    picked = jnp.where(jnp.arange(plan.shape[0]) == step_index[0], plan, 0)
    time_value = jnp.sum(picked).astype(F32)
    half_width = w_mod.shape[0] // 2
    frequency = jnp.exp(-math.log(10000.0) * jnp.arange(half_width, dtype=F32) / half_width)
    angles = time_value * frequency
    embed = jnp.concatenate([jnp.cos(angles), jnp.sin(angles)])
    mod = modulate(jax.nn.silu(embed).astype(BF16), w_mod, core)
    shift, scale, gate = mod.reshape(3, 2 * width)

    local_mean = jnp.mean(values, axis=1)
    local_dev = jnp.sum(jnp.square(values - local_mean[:, None]), axis=1)
    far_mean, far_dev = shift_by(jnp.stack([local_mean, local_dev]), "core", 1)
    average = 0.5 * (local_mean + far_mean)
    spread = (
        local_dev + far_dev + jnp.square(local_mean - far_mean) * (0.5 * width * 2)
    ) / full_width
    normed = (
        (values - average[:, None]) * lax.rsqrt(spread + 1e-06)[:, None] * (1.0 + scale) + shift
    ).astype(BF16)

    halves = [slice(0, rows // 2), slice(rows // 2, rows)]

    def flat(blocks):
        return blocks.reshape(-1, 2 * width)

    normed_all, activs, slopes, deltas, squares = [], [], [], [], 0.0
    for part in halves:
        whole = flat(gather_plane(normed[part]))
        hidden = dot(whole, up, 1, 1)
        hidden = hidden + other_core(hidden)
        activ = jax.nn.gelu(hidden, approximate=True).astype(BF16)
        activ, slope = lax.optimization_barrier((activ, gelu_slope(hidden)))
        line = activ.reshape(4, -1, 4 * piece)
        mixed = {s: dot(line[s], down, 1, 0).astype(BF16) for s in (1, 3, 2, 0)}
        mixed = sum_line(mixed, True).astype(BF16)
        mixed = sum_line(mixed.reshape(4, -1, 2 * width), False)
        residual = values[part] + gate * mixed - goal[part]
        squares = squares + jnp.sum(residual * residual, keepdims=True)
        normed_all.append(whole)
        activs.append(activ)
        slopes.append(slope)
        deltas.append((gate * residual * (1.0 / math.sqrt(token_count))).astype(BF16))

    squares = jnp.broadcast_to(squares, (8, 128))
    squares = (squares + shift_by(squares, "core", 1))[:1, :1]
    extra = as_triple(squares, 3 * place, (16, width))

    delta_all, delta_hidden = [], []
    for half, delta in enumerate(deltas):
        whole = flat(gather_plane(delta))
        if half == 1:
            whole, extra = lax.optimization_barrier((whole, extra))
        hidden_grad = dot(whole, down, 1, 1)
        hidden_grad = hidden_grad + other_core(hidden_grad)
        delta_all.append(whole)
        delta_hidden.append((hidden_grad * slopes[half]).astype(BF16))

    def weight_grad(left, right):
        return [
            sum(dot(a, b[:, h * width : (h + 1) * width], 0, 0) for a, b in zip(left, right)).astype(BF16)
            for h in (0, 1)
        ]

    up_grad = jnp.stack(weight_grad(delta_hidden, normed_all)).reshape(2, 2, 2, piece, width)
    kept = lax.dynamic_index_in_dim(up_grad, core, 2, keepdims=False)
    given = shift_by(lax.dynamic_index_in_dim(up_grad, 1 - core, 2, keepdims=False), "core", 1)
    up_blocks = jnp.stack(by_core(kept, given), axis=2)
    up_blocks = jnp.swapaxes(up_blocks, 0, 1).reshape(8, piece, width)

    down_blocks = jnp.concatenate(weight_grad(activs, delta_all)).reshape(8, piece, width)
    extra = jnp.broadcast_to(extra, (8, 16, width))
    grad_down = jnp.concatenate([down_blocks, extra], axis=1).reshape(-1, width)
    grad_down = lax.psum_scatter(grad_down, DEPTH, scatter_dimension=0, tiled=True)
    squares = jnp.sum(grad_down[piece : piece + 1, :24].astype(F32), keepdims=True)
    grad_down = grad_down[:piece]

    grad_up = sum_depth(up_blocks, place).T.reshape(16, -1, piece)
    share = grad_up.shape[1]
    note = as_triple(squares[None], 0, (16, 16, piece))
    grad_up = lax.all_to_all(
        jnp.concatenate([grad_up, note], axis=1), PLANE, split_axis=0, concat_axis=0, tiled=True
    )
    mean_loss = jnp.sum(grad_up[:, share, :3].astype(F32)) / (token_count * full_width)
    grad_up = jnp.swapaxes(grad_up[:, :share], 0, 1).reshape(share, -1)
    return mean_loss, grad_up, grad_down


def solution(mesh):
    fine = Mesh(mesh.devices.reshape([SIZES[name] for name in AXES]), AXES)
    token_spec = P(("y", "x", "zl"), ("zh", "core"))
    weight_spec = P("zl", ("zh", "core"))
    grad_spec = P(("zl", "y", "x"), ("zh", "core"))
    return jax.shard_map(
        per_device,
        mesh=fine,
        in_specs=(token_spec, token_spec, P(PLANE), P(), P(), weight_spec, weight_spec),
        out_specs=(P(), grad_spec, grad_spec),
        check_vma=False,
    )
```

```python
import math

import jax
import jax.numpy as jnp
from jax import lax
from jax.experimental import pallas as pl
from jax.experimental.pallas import tpu as pltpu
from jax.sharding import Mesh, PartitionSpec as P

GELU_COEF = math.sqrt(2.0 / math.pi)
CUBIC_COEF = 0.044715
AXES = ("y", "x", "zh", "core", "zl")
SIZES = dict(zip(AXES, (4, 4, 2, 2, 4)))
PLANE = ("y", "x")
DEPTH = ("zh", "zl")
F32 = jnp.float32
BF16 = jnp.bfloat16


def gelu_slope(hidden):
    inner = GELU_COEF * (hidden + CUBIC_COEF * hidden * hidden * hidden)
    tanh_value = jnp.tanh(inner)
    return 0.5 * (1.0 + tanh_value) + 0.5 * hidden * (1.0 - tanh_value * tanh_value) * GELU_COEF * (
        1.0 + 3.0 * CUBIC_COEF * hidden * hidden
    )


def shift_by(value, axis, offset):
    names = (axis,) if isinstance(axis, str) else axis
    count = math.prod(SIZES[name] for name in names)
    return lax.ppermute(value, axis, [(i, (i + offset) % count) for i in range(count)])


def turn_by(value, offset, turn):
    ny, nx = SIZES["y"], SIZES["x"]

    def index(y, x, core):
        return ((y % ny) * nx + x % nx) * 2 + core

    pairs = []
    for y in range(ny):
        for x in range(nx):
            for core in range(2):
                along_x = (core == 0) != turn
                goal = index(y, x + offset, core) if along_x else index(y + offset, x, core)
                pairs.append((index(y, x, core), goal))
    return lax.ppermute(value, ("y", "x", "core"), pairs)


def gather_line(value, turn):
    one, three, two = (turn_by(value, s, turn) for s in (1, 3, 2))
    return jnp.stack([value, one, two, three])


def gather_plane(value):
    return gather_line(gather_line(value, False), True)


def sum_line(blocks, turn):
    parts = [turn_by(blocks[s], -s, turn) for s in (1, 3, 2)]
    return blocks[0].astype(F32) + parts[0].astype(F32) + parts[1].astype(F32) + parts[2].astype(F32)


def other_core(value):
    far = shift_by(value, "core", 1)
    return far.reshape(4, 4, -1, far.shape[1]).swapaxes(0, 1).reshape(far.shape)


def triple(value, lane):
    high = value.astype(BF16).astype(F32)
    middle = (value - high).astype(BF16).astype(F32)
    low = value - high - middle
    terms = jnp.where(lane == 0, high, jnp.where(lane == 1, middle, low))
    return jnp.where((lane >= 0) & (lane < 3), terms, 0.0).astype(BF16)


def encode(own, far, place, width):
    def body(place_ref, own_ref, far_ref, out_ref):
        value = jnp.broadcast_to(own_ref[0:1, 0:1] + far_ref[0:1, 0:1], (16, width))
        lane = lax.broadcasted_iota(jnp.int32, (16, width), 1) - 3 * place_ref[0]
        out_ref[...] = triple(value, lane)

    return pl.pallas_call(
        body,
        in_specs=[pl.BlockSpec(memory_space=pltpu.SMEM)] + [pl.BlockSpec(memory_space=pltpu.VMEM)] * 2,
        out_specs=pl.BlockSpec(memory_space=pltpu.VMEM),
        out_shape=jax.ShapeDtypeStruct((16, width), BF16),
        cost_estimate=pl.CostEstimate(flops=16 * width, bytes_accessed=48 * width, transcendentals=0),
        name="encode",
    )(place.reshape(1).astype(jnp.int32), own, far)


def finish(own, up, down):
    piece = (own.shape[0] - 16) // 2
    width = own.shape[1]
    share = width // 16

    def body(own_ref, up_ref, down_ref, grad_ref, send_ref):
        def total(first, last):
            return (
                own_ref[first:last].astype(F32)
                + up_ref[first:last].astype(F32)
                + down_ref[first:last].astype(F32)
            )

        grad_ref[...] = total(0, piece).astype(BF16)
        turned = total(piece, 2 * piece).T.astype(BF16)
        squares = jnp.sum(total(2 * piece, 2 * piece + 16)[0:1], axis=1, keepdims=True)
        lane = lax.broadcasted_iota(jnp.int32, (16, piece), 1)
        note = triple(jnp.broadcast_to(squares, (16, piece)), lane)
        for p in range(16):
            send_ref[p, 0:share] = turned[p * share : (p + 1) * share]
            send_ref[p, share : share + 16] = note

    return pl.pallas_call(
        body,
        in_specs=[pl.BlockSpec(memory_space=pltpu.VMEM)] * 3,
        out_specs=[pl.BlockSpec(memory_space=pltpu.VMEM)] * 2,
        out_shape=[
            jax.ShapeDtypeStruct((piece, width), BF16),
            jax.ShapeDtypeStruct((16, share + 16, piece), BF16),
        ],
        cost_estimate=pl.CostEstimate(
            flops=4 * own.size, bytes_accessed=10 * own.size, transcendentals=0
        ),
        name="finish",
    )(own, up, down)


def gather_depth(value, place):
    half = value.shape[0] // 2
    up, down = [value], [value]
    for _ in range(3):
        up.append(shift_by(up[-1], DEPTH, 1))
        down.append(shift_by(down[-1], DEPTH, -1))
    far = [shift_by(up[-1][:half], DEPTH, 1), shift_by(down[-1][half:], DEPTH, -1)]
    ring = jnp.stack([value, down[1], down[2], down[3], jnp.concatenate(far), up[3], up[2], up[1]])

    def block(z):
        index = jnp.bitwise_and(z - place, 7).astype(jnp.uint32)
        return lax.dynamic_index_in_dim(ring, index, 0, keepdims=False)

    return block


def modulate(level, w_mod, core):
    width = w_mod.shape[1] // 12
    depth = w_mod.shape[0]

    def body(core_ref, level_ref, w_ref, out_ref):
        out_ref[...] = jnp.dot(level_ref[...], w_ref[...], preferred_element_type=F32)

    return pl.pallas_call(
        body,
        grid_spec=pltpu.PrefetchScalarGridSpec(
            num_scalar_prefetch=1,
            grid=(6,),
            in_specs=[
                pl.BlockSpec((16, depth), lambda j, core_ref: (0, 0)),
                pl.BlockSpec(
                    (depth, width), lambda j, core_ref: (0, (j // 2) * 4 + (j % 2) * 2 + core_ref[0])
                ),
            ],
            out_specs=pl.BlockSpec((16, width), lambda j, core_ref: (0, j)),
        ),
        out_shape=jax.ShapeDtypeStruct((16, 6 * width), F32),
        cost_estimate=pl.CostEstimate(
            flops=2 * 16 * depth * 6 * width, bytes_accessed=2 * depth * 6 * width, transcendentals=0
        ),
        name="modulate",
    )(core.reshape(1).astype(jnp.int32), jnp.broadcast_to(level, (16, depth)), w_mod)[0]


def sum_depth(down_blocks, up_blocks, extra, place):
    half = down_blocks.shape[1]

    def block(offset):
        index = jnp.bitwise_and(place + offset, 7).astype(jnp.uint32)
        pair = [
            lax.dynamic_index_in_dim(blocks, index, 0, keepdims=False)
            for blocks in (down_blocks, up_blocks)
        ]
        return jnp.concatenate(pair + [extra])

    def add(a, b):
        return (a.astype(F32) + b.astype(F32)).astype(BF16)

    far = block(4)
    up = shift_by(far[:half], DEPTH, 1)
    down = shift_by(far[half:], DEPTH, -1)
    mine = block(3)
    up = jnp.concatenate([add(mine[:half], up), mine[half:]])
    mine = block(-3)
    down = jnp.concatenate([mine[:half], add(mine[half:], down)])
    up = shift_by(up, DEPTH, 1)
    down = shift_by(down, DEPTH, -1)
    for offset in (2, 1):
        up = shift_by(add(block(offset), up), DEPTH, 1)
        down = shift_by(add(block(-offset), down), DEPTH, -1)
    return finish(block(0), up, down)


def dot(a, b, ca, cb):
    return lax.dot_general(a, b, (((ca,), (cb,)), ((), ())), preferred_element_type=F32)


def per_device(tokens, target, step_index, plan, w_mod, w_up, w_down):
    z_half = lax.axis_index("zh")
    core = lax.axis_index("core")
    place = lax.axis_index(DEPTH)
    group = lax.axis_index(PLANE)
    width = tokens.shape[1]
    rows = tokens.shape[0] // 2
    full_width = 4 * width
    token_count = tokens.shape[0] * 64
    piece = w_down.shape[0] // 16

    def by_core(own, other):
        return jnp.where(core == 0, own, other), jnp.where(core == 0, other, own)

    up_part = lax.dynamic_slice_in_dim(w_up, group * piece, piece, 1).T
    down_part = lax.dynamic_slice_in_dim(w_down, group * piece, piece, 0)
    weights = gather_depth(jnp.concatenate([up_part, down_part]), place)
    down = jnp.concatenate(
        [jnp.concatenate([weights(4 * h + c)[piece:] for c in range(4)]) for h in (0, 1)], axis=1
    )

    def up_half(which):
        return jnp.stack(
            [jnp.stack([weights(4 * h + 2 * c + which)[:piece] for c in (0, 1)]) for h in (0, 1)]
        )

    kept = up_half(core)
    given = shift_by(up_half(1 - core), "core", 1)
    up_pair = by_core(kept, given)
    up = jnp.concatenate(
        [
            jnp.stack([up_pair[0][:, h], up_pair[1][:, h]], axis=1).reshape(4 * piece, width)
            for h in (0, 1)
        ],
        axis=1,
    )

    both = jnp.stack([tokens.reshape(2, rows, width), target.reshape(2, rows, width)], axis=1)
    own = lax.dynamic_index_in_dim(both, z_half, 0, keepdims=False)
    other = shift_by(lax.dynamic_index_in_dim(both, 1 - z_half, 0, keepdims=False), "zh", 1)
    joined = jnp.where(
        z_half == 0, jnp.concatenate([own, other], axis=2), jnp.concatenate([other, own], axis=2)
    ).astype(F32)
    values, goal = joined[0], joined[1]

    picked = jnp.where(jnp.arange(plan.shape[0]) == step_index[0], plan, 0)
    time_value = jnp.sum(picked).astype(F32)
    half_width = w_mod.shape[0] // 2
    frequency = jnp.exp(-math.log(10000.0) * jnp.arange(half_width, dtype=F32) / half_width)
    angles = time_value * frequency
    embed = jnp.concatenate([jnp.cos(angles), jnp.sin(angles)])
    mod = modulate(jax.nn.silu(embed).astype(BF16), w_mod, core)
    shift, scale, gate = mod.reshape(3, 2 * width)

    local_mean = jnp.mean(values, axis=1)
    local_dev = jnp.sum(jnp.square(values - local_mean[:, None]), axis=1)
    far_mean, far_dev = shift_by(jnp.stack([local_mean, local_dev]), "core", 1)
    average = 0.5 * (local_mean + far_mean)
    spread = (
        local_dev + far_dev + jnp.square(local_mean - far_mean) * (0.5 * width * 2)
    ) / full_width
    normed = (
        (values - average[:, None]) * lax.rsqrt(spread + 1e-06)[:, None] * (1.0 + scale) + shift
    ).astype(BF16)

    normed_all = gather_plane(normed).reshape(16 * rows, 2 * width)
    hidden = dot(normed_all, up, 1, 1)
    hidden = hidden + other_core(hidden)
    activ = jax.nn.gelu(hidden, approximate=True).astype(BF16)
    activ, slope = lax.optimization_barrier((activ, gelu_slope(hidden)))
    line = activ.reshape(4, 4 * rows, 4 * piece)
    mixed = {s: dot(line[s], down, 1, 0).astype(BF16) for s in (1, 3, 2, 0)}
    mixed = sum_line(mixed, True).astype(BF16)
    mixed = sum_line(mixed.reshape(4, rows, 2 * width), False)
    residual = values + gate * mixed - goal
    squares = jnp.broadcast_to(jnp.sum(residual * residual, keepdims=True), (8, 128))
    extra = encode(squares, shift_by(squares, "core", 1), place, width)
    delta = (gate * residual * (1.0 / math.sqrt(token_count))).astype(BF16)

    delta_all = gather_plane(delta).reshape(16 * rows, 2 * width)
    delta_all, extra = lax.optimization_barrier((delta_all, extra))
    hidden_grad = dot(delta_all, down, 1, 1)
    hidden_grad = hidden_grad + other_core(hidden_grad)
    down_blocks = jnp.concatenate(
        [dot(activ, delta_all[:, h * width : (h + 1) * width], 0, 0).astype(BF16) for h in (0, 1)]
    ).reshape(8, piece, width)
    delta_hidden = (hidden_grad * slope).astype(BF16)
    up_grad = jnp.stack(
        [dot(delta_hidden, normed_all[:, h * width : (h + 1) * width], 0, 0).astype(BF16) for h in (0, 1)]
    ).reshape(2, 2, 2, piece, width)
    kept = lax.dynamic_index_in_dim(up_grad, core, 2, keepdims=False)
    given = shift_by(lax.dynamic_index_in_dim(up_grad, 1 - core, 2, keepdims=False), "core", 1)
    pair = by_core(kept, given)
    up_blocks = jnp.stack(pair, axis=2)
    up_blocks = jnp.swapaxes(up_blocks, 0, 1).reshape(8, piece, width)

    grad_down, grad_up = sum_depth(down_blocks, up_blocks, extra, place)
    share = width // 16
    grad_up = lax.all_to_all(grad_up, PLANE, split_axis=0, concat_axis=0, tiled=True)
    mean_loss = jnp.sum(grad_up[:, share, :3].astype(F32)) / (token_count * full_width)
    grad_up = jnp.swapaxes(grad_up[:, :share], 0, 1).reshape(share, -1)
    return mean_loss, grad_up, grad_down


def solution(mesh):
    fine = Mesh(mesh.devices.reshape([SIZES[name] for name in AXES]), AXES)
    token_spec = P(("y", "x", "zl"), ("zh", "core"))
    weight_spec = P("zl", ("zh", "core"))
    grad_spec = P(("zl", "y", "x"), ("zh", "core"))
    return jax.shard_map(
        per_device,
        mesh=fine,
        in_specs=(token_spec, token_spec, P(PLANE), P(), P(), weight_spec, weight_spec),
        out_specs=(P(), grad_spec, grad_spec),
        check_vma=False,
    )
```

```python
import math

import jax
import jax.numpy as jnp
from jax import lax
from jax.experimental import pallas as pl
from jax.experimental.pallas import tpu as pltpu
from jax.sharding import Mesh, PartitionSpec as P

GELU_COEF = math.sqrt(2.0 / math.pi)
CUBIC_COEF = 0.044715
AXES = ("y", "x", "zh", "core", "zl")
SIZES = dict(zip(AXES, (4, 4, 2, 2, 4)))
PLANE = ("y", "x")
DEPTH = ("zh", "zl")
F32 = jnp.float32
BF16 = jnp.bfloat16


def gelu_slope(hidden):
    inner = GELU_COEF * (hidden + CUBIC_COEF * hidden * hidden * hidden)
    tanh_value = jnp.tanh(inner)
    return 0.5 * (1.0 + tanh_value) + 0.5 * hidden * (1.0 - tanh_value * tanh_value) * GELU_COEF * (
        1.0 + 3.0 * CUBIC_COEF * hidden * hidden
    )


def shift_by(value, axis, offset):
    names = (axis,) if isinstance(axis, str) else axis
    count = math.prod(SIZES[name] for name in names)
    return lax.ppermute(value, axis, [(i, (i + offset) % count) for i in range(count)])


def turn_by(value, offset, turn):
    ny, nx = SIZES["y"], SIZES["x"]

    def index(y, x, core):
        return ((y % ny) * nx + x % nx) * 2 + core

    pairs = []
    for y in range(ny):
        for x in range(nx):
            for core in range(2):
                along_x = (core == 0) != turn
                goal = index(y, x + offset, core) if along_x else index(y + offset, x, core)
                pairs.append((index(y, x, core), goal))
    return lax.ppermute(value, ("y", "x", "core"), pairs)


def gather_line(value, turn):
    one, three, two = (turn_by(value, s, turn) for s in (1, 3, 2))
    return jnp.stack([value, one, two, three])


def gather_plane(value):
    return gather_line(gather_line(value, False), True)


def sum_line(blocks, turn):
    parts = [turn_by(blocks[s], -s, turn) for s in (1, 3, 2)]
    return blocks[0].astype(F32) + parts[0].astype(F32) + parts[1].astype(F32) + parts[2].astype(F32)


def other_core(value):
    far = shift_by(value, "core", 1)
    return far.reshape(4, 4, -1, far.shape[1]).swapaxes(0, 1).reshape(far.shape)


def triple(value, lane):
    high = value.astype(BF16).astype(F32)
    middle = (value - high).astype(BF16).astype(F32)
    low = value - high - middle
    terms = jnp.where(lane == 0, high, jnp.where(lane == 1, middle, low))
    return jnp.where((lane >= 0) & (lane < 3), terms, 0.0).astype(BF16)


def encode(own, far, place, width):
    def body(place_ref, own_ref, far_ref, out_ref):
        value = jnp.broadcast_to(own_ref[0:1, 0:1] + far_ref[0:1, 0:1], (16, width))
        lane = lax.broadcasted_iota(jnp.int32, (16, width), 1) - 3 * place_ref[0]
        out_ref[...] = triple(value, lane)

    return pl.pallas_call(
        body,
        in_specs=[pl.BlockSpec(memory_space=pltpu.SMEM)] + [pl.BlockSpec(memory_space=pltpu.VMEM)] * 2,
        out_specs=pl.BlockSpec(memory_space=pltpu.VMEM),
        out_shape=jax.ShapeDtypeStruct((16, width), BF16),
        cost_estimate=pl.CostEstimate(flops=16 * width, bytes_accessed=48 * width, transcendentals=0),
        name="encode",
    )(place.reshape(1).astype(jnp.int32), own, far)


def finish(own, up, down):
    piece = (own.shape[0] - 16) // 2
    width = own.shape[1]
    share = width // 16

    def body(own_ref, up_ref, down_ref, grad_ref, send_ref):
        def total(first, last):
            return (
                own_ref[first:last].astype(F32)
                + up_ref[first:last].astype(F32)
                + down_ref[first:last].astype(F32)
            )

        grad_ref[...] = total(0, piece).astype(BF16)
        turned = total(piece, 2 * piece).T.astype(BF16)
        squares = jnp.sum(total(2 * piece, 2 * piece + 16)[0:1], axis=1, keepdims=True)
        lane = lax.broadcasted_iota(jnp.int32, (16, piece), 1)
        note = triple(jnp.broadcast_to(squares, (16, piece)), lane)
        for p in range(16):
            send_ref[p, 0:share] = turned[p * share : (p + 1) * share]
            send_ref[p, share : share + 16] = note

    return pl.pallas_call(
        body,
        in_specs=[pl.BlockSpec(memory_space=pltpu.VMEM)] * 3,
        out_specs=[pl.BlockSpec(memory_space=pltpu.VMEM)] * 2,
        out_shape=[
            jax.ShapeDtypeStruct((piece, width), BF16),
            jax.ShapeDtypeStruct((16, share + 16, piece), BF16),
        ],
        cost_estimate=pl.CostEstimate(
            flops=4 * own.size, bytes_accessed=10 * own.size, transcendentals=0
        ),
        name="finish",
    )(own, up, down)


def gather_depth(value, place):
    half = value.shape[0] // 2
    up, down = [value], [value]
    for _ in range(3):
        up.append(shift_by(up[-1], DEPTH, 1))
        down.append(shift_by(down[-1], DEPTH, -1))
    far = [shift_by(up[-1][:half], DEPTH, 1), shift_by(down[-1][half:], DEPTH, -1)]
    ring = jnp.stack([value, down[1], down[2], down[3], jnp.concatenate(far), up[3], up[2], up[1]])

    def block(z):
        index = jnp.bitwise_and(z - place, 7).astype(jnp.uint32)
        return lax.dynamic_index_in_dim(ring, index, 0, keepdims=False)

    return block


def modulate(level, w_mod, core):
    width = w_mod.shape[1] // 12
    depth = w_mod.shape[0]

    def body(core_ref, level_ref, w_ref, out_ref):
        out_ref[...] = jnp.dot(level_ref[...], w_ref[...], preferred_element_type=F32)

    return pl.pallas_call(
        body,
        grid_spec=pltpu.PrefetchScalarGridSpec(
            num_scalar_prefetch=1,
            grid=(6,),
            in_specs=[
                pl.BlockSpec((16, depth), lambda j, core_ref: (0, 0)),
                pl.BlockSpec(
                    (depth, width), lambda j, core_ref: (0, (j // 2) * 4 + (j % 2) * 2 + core_ref[0])
                ),
            ],
            out_specs=pl.BlockSpec((16, width), lambda j, core_ref: (0, j)),
        ),
        out_shape=jax.ShapeDtypeStruct((16, 6 * width), F32),
        cost_estimate=pl.CostEstimate(
            flops=2 * 16 * depth * 6 * width, bytes_accessed=2 * depth * 6 * width, transcendentals=0
        ),
        name="modulate",
    )(core.reshape(1).astype(jnp.int32), jnp.broadcast_to(level, (16, depth)), w_mod)[0]


def sum_depth(down_blocks, up_blocks, extra, place):
    half = down_blocks.shape[1]

    def block(offset):
        index = jnp.bitwise_and(place + offset, 7).astype(jnp.uint32)
        pair = [
            lax.dynamic_index_in_dim(blocks, index, 0, keepdims=False)
            for blocks in (down_blocks, up_blocks)
        ]
        return jnp.concatenate(pair + [extra])

    def add(a, b):
        return (a.astype(F32) + b.astype(F32)).astype(BF16)

    far = block(4)
    up = shift_by(far[:half], DEPTH, 1)
    down = shift_by(far[half:], DEPTH, -1)
    mine = block(3)
    up = jnp.concatenate([add(mine[:half], up), mine[half:]])
    mine = block(-3)
    down = jnp.concatenate([mine[:half], add(mine[half:], down)])
    up = shift_by(up, DEPTH, 1)
    down = shift_by(down, DEPTH, -1)
    for offset in (2, 1):
        up = shift_by(add(block(offset), up), DEPTH, 1)
        down = shift_by(add(block(-offset), down), DEPTH, -1)
    return finish(block(0), up, down)


def dot(a, b, ca, cb):
    return lax.dot_general(a, b, (((ca,), (cb,)), ((), ())), preferred_element_type=F32)


def per_device(tokens, target, step_index, plan, w_mod, w_up, w_down):
    z_half = lax.axis_index("zh")
    core = lax.axis_index("core")
    place = lax.axis_index(DEPTH)
    group = lax.axis_index(PLANE)
    width = tokens.shape[1]
    rows = tokens.shape[0] // 2
    full_width = 4 * width
    token_count = tokens.shape[0] * 64
    piece = w_down.shape[0] // 16

    def by_core(own, other):
        return jnp.where(core == 0, own, other), jnp.where(core == 0, other, own)

    up_part = lax.dynamic_slice_in_dim(w_up, group * piece, piece, 1).T
    down_part = lax.dynamic_slice_in_dim(w_down, group * piece, piece, 0)
    both = jnp.stack([tokens.reshape(2, rows, width), target.reshape(2, rows, width)], axis=1)
    own = lax.dynamic_index_in_dim(both, z_half, 0, keepdims=False)
    other = shift_by(lax.dynamic_index_in_dim(both, 1 - z_half, 0, keepdims=False), "zh", 1)
    other, part = lax.optimization_barrier((other, jnp.concatenate([up_part, down_part])))
    joined = jnp.where(
        z_half == 0, jnp.concatenate([own, other], axis=2), jnp.concatenate([other, own], axis=2)
    ).astype(F32)
    values, goal = joined[0], joined[1]

    picked = jnp.where(jnp.arange(plan.shape[0]) == step_index[0], plan, 0)
    time_value = jnp.sum(picked).astype(F32)
    half_width = w_mod.shape[0] // 2
    frequency = jnp.exp(-math.log(10000.0) * jnp.arange(half_width, dtype=F32) / half_width)
    angles = time_value * frequency
    embed = jnp.concatenate([jnp.cos(angles), jnp.sin(angles)])
    mod = modulate(jax.nn.silu(embed).astype(BF16), w_mod, core)
    weights = gather_depth(part, place)
    down = jnp.concatenate(
        [jnp.concatenate([weights(4 * h + c)[piece:] for c in range(4)]) for h in (0, 1)], axis=1
    )

    def up_half(which):
        return jnp.stack(
            [jnp.stack([weights(4 * h + 2 * c + which)[:piece] for c in (0, 1)]) for h in (0, 1)]
        )

    kept = up_half(core)
    given = shift_by(up_half(1 - core), "core", 1)
    up_pair = by_core(kept, given)
    up = jnp.concatenate(
        [
            jnp.stack([up_pair[0][:, h], up_pair[1][:, h]], axis=1).reshape(4 * piece, width)
            for h in (0, 1)
        ],
        axis=1,
    )

    shift, scale, gate = mod.reshape(3, 2 * width)

    local_mean = jnp.mean(values, axis=1)
    local_dev = jnp.sum(jnp.square(values - local_mean[:, None]), axis=1)
    far_mean, far_dev = shift_by(jnp.stack([local_mean, local_dev]), "core", 1)
    average = 0.5 * (local_mean + far_mean)
    spread = (
        local_dev + far_dev + jnp.square(local_mean - far_mean) * (0.5 * width * 2)
    ) / full_width
    normed = (
        (values - average[:, None]) * lax.rsqrt(spread + 1e-06)[:, None] * (1.0 + scale) + shift
    ).astype(BF16)

    normed_all = gather_plane(normed).reshape(16 * rows, 2 * width)
    hidden = dot(normed_all, up, 1, 1)
    hidden = hidden + other_core(hidden)
    activ = jax.nn.gelu(hidden, approximate=True).astype(BF16)
    activ, slope = lax.optimization_barrier((activ, gelu_slope(hidden)))
    line = activ.reshape(4, 4 * rows, 4 * piece)
    mixed = {s: dot(line[s], down, 1, 0).astype(BF16) for s in (1, 3, 2, 0)}
    mixed = sum_line(mixed, True).astype(BF16)
    mixed = sum_line(mixed.reshape(4, rows, 2 * width), False)
    residual = values + gate * mixed - goal
    squares = jnp.broadcast_to(jnp.sum(residual * residual, keepdims=True), (8, 128))
    extra = encode(squares, shift_by(squares, "core", 1), place, width)
    delta = (gate * residual * (1.0 / math.sqrt(token_count))).astype(BF16)

    delta_all = gather_plane(delta).reshape(16 * rows, 2 * width)
    delta_all, extra = lax.optimization_barrier((delta_all, extra))
    hidden_grad = dot(delta_all, down, 1, 1)
    far = other_core(hidden_grad)
    down_blocks = jnp.concatenate(
        [dot(activ, delta_all[:, h * width : (h + 1) * width], 0, 0).astype(BF16) for h in (0, 1)]
    ).reshape(8, piece, width)
    far, down_blocks = lax.optimization_barrier((far, down_blocks))
    hidden_grad = hidden_grad + far
    delta_hidden = (hidden_grad * slope).astype(BF16)
    up_grad = jnp.stack(
        [dot(delta_hidden, normed_all[:, h * width : (h + 1) * width], 0, 0).astype(BF16) for h in (0, 1)]
    ).reshape(2, 2, 2, piece, width)
    kept = lax.dynamic_index_in_dim(up_grad, core, 2, keepdims=False)
    given = shift_by(lax.dynamic_index_in_dim(up_grad, 1 - core, 2, keepdims=False), "core", 1)
    pair = by_core(kept, given)
    up_blocks = jnp.stack(pair, axis=2)
    up_blocks = jnp.swapaxes(up_blocks, 0, 1).reshape(8, piece, width)

    grad_down, grad_up = sum_depth(down_blocks, up_blocks, extra, place)
    share = width // 16
    grad_up = lax.all_to_all(grad_up, PLANE, split_axis=0, concat_axis=0, tiled=True)
    mean_loss = jnp.sum(grad_up[:, share, :3].astype(F32)) / (token_count * full_width)
    grad_up = jnp.swapaxes(grad_up[:, :share], 0, 1).reshape(share, -1)
    return mean_loss, grad_up, grad_down


def solution(mesh):
    fine = Mesh(mesh.devices.reshape([SIZES[name] for name in AXES]), AXES)
    token_spec = P(("y", "x", "zl"), ("zh", "core"))
    weight_spec = P("zl", ("zh", "core"))
    grad_spec = P(("zl", "y", "x"), ("zh", "core"))
    return jax.shard_map(
        per_device,
        mesh=fine,
        in_specs=(token_spec, token_spec, P(PLANE), P(), P(), weight_spec, weight_spec),
        out_specs=(P(), grad_spec, grad_spec),
        check_vma=False,
    )
```

```python
import math

import jax
import jax.numpy as jnp
from jax import lax
from jax.experimental import pallas as pl
from jax.experimental.pallas import tpu as pltpu
from jax.sharding import Mesh, PartitionSpec as P

GELU_COEF = math.sqrt(2.0 / math.pi)
CUBIC_COEF = 0.044715
AXES = ("y", "x", "zh", "core", "zl")
SIZES = dict(zip(AXES, (4, 4, 2, 2, 4)))
PLANE = ("y", "x")
DEPTH = ("zh", "zl")
F32 = jnp.float32
BF16 = jnp.bfloat16


def gelu_slope(hidden):
    inner = GELU_COEF * (hidden + CUBIC_COEF * hidden * hidden * hidden)
    tanh_value = jnp.tanh(inner)
    return 0.5 * (1.0 + tanh_value) + 0.5 * hidden * (1.0 - tanh_value * tanh_value) * GELU_COEF * (
        1.0 + 3.0 * CUBIC_COEF * hidden * hidden
    )


def shift_by(value, axis, offset):
    names = (axis,) if isinstance(axis, str) else axis
    count = math.prod(SIZES[name] for name in names)
    return lax.ppermute(value, axis, [(i, (i + offset) % count) for i in range(count)])


def turn_by(value, offset, turn):
    ny, nx = SIZES["y"], SIZES["x"]

    def index(y, x, core):
        return ((y % ny) * nx + x % nx) * 2 + core

    pairs = []
    for y in range(ny):
        for x in range(nx):
            for core in range(2):
                along_x = (core == 0) != turn
                goal = index(y, x + offset, core) if along_x else index(y + offset, x, core)
                pairs.append((index(y, x, core), goal))
    return lax.ppermute(value, ("y", "x", "core"), pairs)


def gather_line(value, turn):
    one, three, two = (turn_by(value, s, turn) for s in (1, 3, 2))
    return jnp.stack([value, one, two, three])


def gather_plane(value):
    return gather_line(gather_line(value, False), True)


def sum_line(blocks, turn):
    parts = [turn_by(blocks[s], -s, turn) for s in (1, 3, 2)]
    return blocks[0].astype(F32) + parts[0].astype(F32) + parts[1].astype(F32) + parts[2].astype(F32)


def other_core(value):
    far = shift_by(value, "core", 1)
    return far.reshape(4, 4, -1, far.shape[1]).swapaxes(0, 1).reshape(far.shape)


def triple(value, lane):
    high = value.astype(BF16).astype(F32)
    middle = (value - high).astype(BF16).astype(F32)
    low = value - high - middle
    terms = jnp.where(lane == 0, high, jnp.where(lane == 1, middle, low))
    return jnp.where((lane >= 0) & (lane < 3), terms, 0.0).astype(BF16)


def encode(own, far, place, width):
    def body(place_ref, own_ref, far_ref, out_ref):
        value = jnp.broadcast_to(own_ref[0:1, 0:1] + far_ref[0:1, 0:1], (16, width))
        lane = lax.broadcasted_iota(jnp.int32, (16, width), 1) - 3 * place_ref[0]
        out_ref[...] = triple(value, lane)

    return pl.pallas_call(
        body,
        in_specs=[pl.BlockSpec(memory_space=pltpu.SMEM)] + [pl.BlockSpec(memory_space=pltpu.VMEM)] * 2,
        out_specs=pl.BlockSpec(memory_space=pltpu.VMEM),
        out_shape=jax.ShapeDtypeStruct((16, width), BF16),
        cost_estimate=pl.CostEstimate(flops=16 * width, bytes_accessed=48 * width, transcendentals=0),
        name="encode",
    )(place.reshape(1).astype(jnp.int32), own, far)


def finish(own, up, down):
    piece = (own.shape[0] - 16) // 2
    width = own.shape[1]
    share = width // 16

    def body(own_ref, up_ref, down_ref, grad_ref, send_ref):
        def total(first, last):
            return (
                own_ref[first:last].astype(F32)
                + up_ref[first:last].astype(F32)
                + down_ref[first:last].astype(F32)
            )

        grad_ref[...] = total(0, piece).astype(BF16)
        turned = total(piece, 2 * piece).T.astype(BF16)
        squares = jnp.sum(total(2 * piece, 2 * piece + 16)[0:1], axis=1, keepdims=True)
        lane = lax.broadcasted_iota(jnp.int32, (16, piece), 1)
        note = triple(jnp.broadcast_to(squares, (16, piece)), lane)
        for p in range(16):
            send_ref[p, 0:share] = turned[p * share : (p + 1) * share]
            send_ref[p, share : share + 16] = note

    return pl.pallas_call(
        body,
        in_specs=[pl.BlockSpec(memory_space=pltpu.VMEM)] * 3,
        out_specs=[pl.BlockSpec(memory_space=pltpu.VMEM)] * 2,
        out_shape=[
            jax.ShapeDtypeStruct((piece, width), BF16),
            jax.ShapeDtypeStruct((16, share + 16, piece), BF16),
        ],
        cost_estimate=pl.CostEstimate(
            flops=4 * own.size, bytes_accessed=10 * own.size, transcendentals=0
        ),
        name="finish",
    )(own, up, down)


def gather_depth(value, place):
    half = value.shape[0] // 2
    up, down = [value], [value]
    for _ in range(3):
        up.append(shift_by(up[-1], DEPTH, 1))
        down.append(shift_by(down[-1], DEPTH, -1))
    far = [shift_by(up[-1][:half], DEPTH, 1), shift_by(down[-1][half:], DEPTH, -1)]
    ring = jnp.stack([value, down[1], down[2], down[3], jnp.concatenate(far), up[3], up[2], up[1]])

    def block(z):
        index = jnp.bitwise_and(z - place, 7).astype(jnp.uint32)
        return lax.dynamic_index_in_dim(ring, index, 0, keepdims=False)

    return block


def modulate(level, w_mod, core):
    width = w_mod.shape[1] // 12
    depth = w_mod.shape[0]

    def body(core_ref, level_ref, w_ref, out_ref):
        out_ref[...] = jnp.dot(level_ref[...], w_ref[...], preferred_element_type=F32)

    return pl.pallas_call(
        body,
        grid_spec=pltpu.PrefetchScalarGridSpec(
            num_scalar_prefetch=1,
            grid=(6,),
            in_specs=[
                pl.BlockSpec((16, depth), lambda j, core_ref: (0, 0)),
                pl.BlockSpec(
                    (depth, width), lambda j, core_ref: (0, (j // 2) * 4 + (j % 2) * 2 + core_ref[0])
                ),
            ],
            out_specs=pl.BlockSpec((16, width), lambda j, core_ref: (0, j)),
        ),
        out_shape=jax.ShapeDtypeStruct((16, 6 * width), F32),
        cost_estimate=pl.CostEstimate(
            flops=2 * 16 * depth * 6 * width, bytes_accessed=2 * depth * 6 * width, transcendentals=0
        ),
        name="modulate",
    )(core.reshape(1).astype(jnp.int32), jnp.broadcast_to(level, (16, depth)), w_mod)[0]


def sum_depth(down_blocks, up_blocks, extra, place):
    half = down_blocks.shape[1]

    def block(offset):
        index = jnp.bitwise_and(place + offset, 7).astype(jnp.uint32)
        pair = [
            lax.dynamic_index_in_dim(blocks, index, 0, keepdims=False)
            for blocks in (down_blocks, up_blocks)
        ]
        return jnp.concatenate(pair + [extra])

    def add(a, b):
        return (a.astype(F32) + b.astype(F32)).astype(BF16)

    far = block(4)
    up = shift_by(far[:half], DEPTH, 1)
    down = shift_by(far[half:], DEPTH, -1)
    mine = block(3)
    up = jnp.concatenate([add(mine[:half], up), mine[half:]])
    mine = block(-3)
    down = jnp.concatenate([mine[:half], add(mine[half:], down)])
    up = shift_by(up, DEPTH, 1)
    down = shift_by(down, DEPTH, -1)
    for offset in (2, 1):
        up = shift_by(add(block(offset), up), DEPTH, 1)
        down = shift_by(add(block(-offset), down), DEPTH, -1)
    return finish(block(0), up, down)


def dot(a, b, ca, cb):
    return lax.dot_general(a, b, (((ca,), (cb,)), ((), ())), preferred_element_type=F32)


def per_device(tokens, target, step_index, plan, w_mod, w_up, w_down):
    z_half = lax.axis_index("zh")
    core = lax.axis_index("core")
    place = lax.axis_index(DEPTH)
    group = lax.axis_index(PLANE)
    width = tokens.shape[1]
    rows = tokens.shape[0] // 2
    full_width = 4 * width
    token_count = tokens.shape[0] * 64
    piece = w_down.shape[0] // 16

    def by_core(own, other):
        return jnp.where(core == 0, own, other), jnp.where(core == 0, other, own)

    up_part = lax.dynamic_slice_in_dim(w_up, group * piece, piece, 1).T
    down_part = lax.dynamic_slice_in_dim(w_down, group * piece, piece, 0)
    both = jnp.stack([tokens.reshape(2, rows, width), target.reshape(2, rows, width)], axis=1)
    own = lax.dynamic_index_in_dim(both, z_half, 0, keepdims=False)
    other = shift_by(lax.dynamic_index_in_dim(both, 1 - z_half, 0, keepdims=False), "zh", 1)
    other, part = lax.optimization_barrier((other, jnp.concatenate([up_part, down_part])))
    joined = jnp.where(
        z_half == 0, jnp.concatenate([own, other], axis=2), jnp.concatenate([other, own], axis=2)
    ).astype(F32)
    values, goal = joined[0], joined[1]

    picked = jnp.where(jnp.arange(plan.shape[0]) == step_index[0], plan, 0)
    time_value = jnp.sum(picked).astype(F32)
    half_width = w_mod.shape[0] // 2
    frequency = jnp.exp(-math.log(10000.0) * jnp.arange(half_width, dtype=F32) / half_width)
    angles = time_value * frequency
    embed = jnp.concatenate([jnp.cos(angles), jnp.sin(angles)])
    mod = modulate(jax.nn.silu(embed).astype(BF16), w_mod, core)
    weights = gather_depth(part, place)
    down = jnp.concatenate(
        [jnp.concatenate([weights(4 * h + c)[piece:] for c in range(4)]) for h in (0, 1)], axis=1
    )

    def up_half(which):
        return jnp.stack(
            [jnp.stack([weights(4 * h + 2 * c + which)[:piece] for c in (0, 1)]) for h in (0, 1)]
        )

    kept = up_half(core)
    given = shift_by(up_half(1 - core), "core", 1)
    up_pair = by_core(kept, given)
    up = jnp.concatenate(
        [
            jnp.stack([up_pair[0][:, h], up_pair[1][:, h]], axis=1).reshape(4 * piece, width)
            for h in (0, 1)
        ],
        axis=1,
    )

    shift, scale, gate = mod.reshape(3, 2 * width)

    local_mean = jnp.mean(values, axis=1)
    local_dev = jnp.sum(jnp.square(values - local_mean[:, None]), axis=1)
    far_mean, far_dev = shift_by(jnp.stack([local_mean, local_dev]), "core", 1)
    average = 0.5 * (local_mean + far_mean)
    spread = (
        local_dev + far_dev + jnp.square(local_mean - far_mean) * (0.5 * width * 2)
    ) / full_width
    normed = (
        (values - average[:, None]) * lax.rsqrt(spread + 1e-06)[:, None] * (1.0 + scale) + shift
    ).astype(BF16)

    normed_all = gather_plane(normed).reshape(16 * rows, 2 * width)
    hidden = dot(normed_all, up, 1, 1).astype(BF16)
    hidden = hidden.astype(F32) + other_core(hidden).astype(F32)
    activ = jax.nn.gelu(hidden, approximate=True).astype(BF16)
    activ, slope = lax.optimization_barrier((activ, gelu_slope(hidden)))
    line = activ.reshape(4, 4 * rows, 4 * piece)
    mixed = {s: dot(line[s], down, 1, 0).astype(BF16) for s in (1, 3, 2, 0)}
    mixed = sum_line(mixed, True).astype(BF16)
    mixed = sum_line(mixed.reshape(4, rows, 2 * width), False)
    residual = values + gate * mixed - goal
    squares = jnp.broadcast_to(jnp.sum(residual * residual, keepdims=True), (8, 128))
    extra = encode(squares, shift_by(squares, "core", 1), place, width)
    delta = (gate * residual * (1.0 / math.sqrt(token_count))).astype(BF16)

    delta_all = gather_plane(delta).reshape(16 * rows, 2 * width)
    delta_all, extra = lax.optimization_barrier((delta_all, extra))
    hidden_grad = dot(delta_all, down, 1, 1).astype(BF16)
    far = other_core(hidden_grad)
    down_blocks = jnp.concatenate(
        [dot(activ, delta_all[:, h * width : (h + 1) * width], 0, 0).astype(BF16) for h in (0, 1)]
    ).reshape(8, piece, width)
    far, down_blocks = lax.optimization_barrier((far, down_blocks))
    hidden_grad = hidden_grad.astype(F32) + far.astype(F32)
    delta_hidden = (hidden_grad * slope).astype(BF16)
    up_grad = jnp.stack(
        [dot(delta_hidden, normed_all[:, h * width : (h + 1) * width], 0, 0).astype(BF16) for h in (0, 1)]
    ).reshape(2, 2, 2, piece, width)
    kept = lax.dynamic_index_in_dim(up_grad, core, 2, keepdims=False)
    given = shift_by(lax.dynamic_index_in_dim(up_grad, 1 - core, 2, keepdims=False), "core", 1)
    pair = by_core(kept, given)
    up_blocks = jnp.stack(pair, axis=2)
    up_blocks = jnp.swapaxes(up_blocks, 0, 1).reshape(8, piece, width)

    grad_down, grad_up = sum_depth(down_blocks, up_blocks, extra, place)
    share = width // 16
    grad_up = lax.all_to_all(grad_up, PLANE, split_axis=0, concat_axis=0, tiled=True)
    mean_loss = jnp.sum(grad_up[:, share, :3].astype(F32)) / (token_count * full_width)
    grad_up = jnp.swapaxes(grad_up[:, :share], 0, 1).reshape(share, -1)
    return mean_loss, grad_up, grad_down


def solution(mesh):
    fine = Mesh(mesh.devices.reshape([SIZES[name] for name in AXES]), AXES)
    token_spec = P(("y", "x", "zl"), ("zh", "core"))
    weight_spec = P("zl", ("zh", "core"))
    grad_spec = P(("zl", "y", "x"), ("zh", "core"))
    return jax.shard_map(
        per_device,
        mesh=fine,
        in_specs=(token_spec, token_spec, P(PLANE), P(), P(), weight_spec, weight_spec),
        out_specs=(P(), grad_spec, grad_spec),
        check_vma=False,
    )
```

```python
import math

import jax
import jax.numpy as jnp
from jax import lax
from jax.experimental import pallas as pl
from jax.experimental.pallas import tpu as pltpu
from jax.sharding import Mesh, PartitionSpec as P

GELU_COEF = math.sqrt(2.0 / math.pi)
CUBIC_COEF = 0.044715
AXES = ("y", "x", "zh", "core", "zl")
SIZES = dict(zip(AXES, (4, 4, 2, 2, 4)))
PLANE = ("y", "x")
DEPTH = ("zh", "zl")
F32 = jnp.float32
BF16 = jnp.bfloat16


def shift_by(value, axis, offset):
    names = (axis,) if isinstance(axis, str) else axis
    count = math.prod(SIZES[name] for name in names)
    return lax.ppermute(value, axis, [(i, (i + offset) % count) for i in range(count)])


def turn_by(value, offset, turn):
    ny, nx = SIZES["y"], SIZES["x"]

    def index(y, x, core):
        return ((y % ny) * nx + x % nx) * 2 + core

    pairs = []
    for y in range(ny):
        for x in range(nx):
            for core in range(2):
                along_x = (core == 0) != turn
                goal = index(y, x + offset, core) if along_x else index(y + offset, x, core)
                pairs.append((index(y, x, core), goal))
    return lax.ppermute(value, ("y", "x", "core"), pairs)


def gather_line(value, turn):
    one, three, two = (turn_by(value, s, turn) for s in (1, 3, 2))
    return jnp.stack([value, one, two, three])


def gather_plane(value):
    return gather_line(gather_line(value, False), True)


def sum_line(blocks, turn):
    parts = [turn_by(blocks[s], -s, turn) for s in (1, 3, 2)]
    return blocks[0].astype(F32) + parts[0].astype(F32) + parts[1].astype(F32) + parts[2].astype(F32)


def local_call(body, outs, *operands, name, cost):
    specs = [
        pl.BlockSpec(memory_space=pltpu.SMEM if value.ndim == 1 else pltpu.VMEM) for value in operands
    ]
    size = sum(value.size * value.dtype.itemsize for value in list(operands) + outs)
    return pl.pallas_call(
        body,
        in_specs=specs,
        out_specs=[pl.BlockSpec(memory_space=pltpu.VMEM)] * len(outs),
        out_shape=outs,
        cost_estimate=pl.CostEstimate(flops=cost, bytes_accessed=size, transcendentals=0),
        compiler_params=pltpu.CompilerParams(vmem_limit_bytes=2 * size + (8 << 20)),
        name=name,
    )(*operands)


def pair_blocks(count):
    step = count // 16
    for i in range(16):
        j = (i % 4) * 4 + i // 4
        yield slice(i * step, (i + 1) * step), slice(j * step, (j + 1) * step)


def activate(own, far):
    def body(own_ref, far_ref, activ_ref, slope_ref):
        for here, there in pair_blocks(own.shape[0]):
            hidden = own_ref[here].astype(F32) + far_ref[there].astype(F32)
            square = hidden * hidden
            tanh_value = jnp.tanh(GELU_COEF * (hidden + CUBIC_COEF * square * hidden))
            half = 0.5 * (1.0 + tanh_value)
            activ_ref[here] = (hidden * half).astype(BF16)
            slope_ref[here] = half + 0.5 * hidden * (1.0 - tanh_value * tanh_value) * GELU_COEF * (
                1.0 + 3.0 * CUBIC_COEF * square
            )

    outs = [jax.ShapeDtypeStruct(own.shape, BF16), jax.ShapeDtypeStruct(own.shape, F32)]
    return local_call(body, outs, own, far, name="activate", cost=20 * own.size)


def slope_grad(own, far, slope):
    def body(own_ref, far_ref, slope_ref, out_ref):
        for here, there in pair_blocks(own.shape[0]):
            total = own_ref[here].astype(F32) + far_ref[there].astype(F32)
            out_ref[here] = (total * slope_ref[here]).astype(BF16)

    outs = [jax.ShapeDtypeStruct(own.shape, BF16)]
    return local_call(body, outs, own, far, slope, name="slope_grad", cost=3 * own.size)[0]


def split_ring(ring, place, core):
    rows, width = ring.shape[1] // 2, ring.shape[2]

    def body(index_ref, ring_ref, kept_ref, given_ref):
        for h in (0, 1):
            for c in (0, 1):
                first = 4 * h + 2 * c - index_ref[0]
                kept_ref[h, c] = ring_ref[jnp.bitwise_and(first + index_ref[1], 7), 0:rows]
                given_ref[h, c] = ring_ref[jnp.bitwise_and(first + 1 - index_ref[1], 7), 0:rows]

    outs = [jax.ShapeDtypeStruct((2, 2, rows, width), BF16)] * 2
    index = jnp.stack([place, core]).astype(jnp.int32)
    return local_call(body, outs, index, ring, name="split_ring", cost=8 * rows * width)


def join_cores(kept, given, core):
    rows, width = kept.shape[2:]

    def body(core_ref, kept_ref, given_ref, out_ref):
        for h in (0, 1):
            for c in (0, 1):
                own = pl.multiple_of((2 * h + core_ref[0]) * rows, 16)
                far = pl.multiple_of((2 * h + 1 - core_ref[0]) * rows, 16)
                columns = slice(c * width, (c + 1) * width)
                out_ref[pl.ds(own, rows), columns] = kept_ref[h, c]
                out_ref[pl.ds(far, rows), columns] = given_ref[h, c]

    outs = [jax.ShapeDtypeStruct((4 * rows, 2 * width), BF16)]
    index = core.reshape(1).astype(jnp.int32)
    return local_call(body, outs, index, kept, given, name="join_cores", cost=8 * rows * width)[0]


def triple(value, lane):
    high = value.astype(BF16).astype(F32)
    middle = (value - high).astype(BF16).astype(F32)
    low = value - high - middle
    terms = jnp.where(lane == 0, high, jnp.where(lane == 1, middle, low))
    return jnp.where((lane >= 0) & (lane < 3), terms, 0.0).astype(BF16)


def encode(own, far, place, width):
    def body(place_ref, own_ref, far_ref, out_ref):
        value = jnp.broadcast_to(own_ref[0:1, 0:1] + far_ref[0:1, 0:1], (16, width))
        lane = lax.broadcasted_iota(jnp.int32, (16, width), 1) - 3 * place_ref[0]
        out_ref[...] = triple(value, lane)

    return pl.pallas_call(
        body,
        in_specs=[pl.BlockSpec(memory_space=pltpu.SMEM)] + [pl.BlockSpec(memory_space=pltpu.VMEM)] * 2,
        out_specs=pl.BlockSpec(memory_space=pltpu.VMEM),
        out_shape=jax.ShapeDtypeStruct((16, width), BF16),
        cost_estimate=pl.CostEstimate(flops=16 * width, bytes_accessed=48 * width, transcendentals=0),
        name="encode",
    )(place.reshape(1).astype(jnp.int32), own, far)


def finish(own, up, down):
    piece = (own.shape[0] - 16) // 2
    width = own.shape[1]
    share = width // 16

    def body(own_ref, up_ref, down_ref, grad_ref, send_ref):
        def total(first, last):
            return (
                own_ref[first:last].astype(F32)
                + up_ref[first:last].astype(F32)
                + down_ref[first:last].astype(F32)
            )

        grad_ref[...] = total(0, piece).astype(BF16)
        turned = total(piece, 2 * piece).T.astype(BF16)
        squares = jnp.sum(total(2 * piece, 2 * piece + 16)[0:1], axis=1, keepdims=True)
        lane = lax.broadcasted_iota(jnp.int32, (16, piece), 1)
        note = triple(jnp.broadcast_to(squares, (16, piece)), lane)
        for p in range(16):
            send_ref[p, 0:share] = turned[p * share : (p + 1) * share]
            send_ref[p, share : share + 16] = note

    return pl.pallas_call(
        body,
        in_specs=[pl.BlockSpec(memory_space=pltpu.VMEM)] * 3,
        out_specs=[pl.BlockSpec(memory_space=pltpu.VMEM)] * 2,
        out_shape=[
            jax.ShapeDtypeStruct((piece, width), BF16),
            jax.ShapeDtypeStruct((16, share + 16, piece), BF16),
        ],
        cost_estimate=pl.CostEstimate(
            flops=4 * own.size, bytes_accessed=10 * own.size, transcendentals=0
        ),
        name="finish",
    )(own, up, down)


def gather_depth(value, place):
    half = value.shape[0] // 2
    up, down = [value], [value]
    for _ in range(3):
        up.append(shift_by(up[-1], DEPTH, 1))
        down.append(shift_by(down[-1], DEPTH, -1))
    far = [shift_by(up[-1][:half], DEPTH, 1), shift_by(down[-1][half:], DEPTH, -1)]
    ring = jnp.stack([value, down[1], down[2], down[3], jnp.concatenate(far), up[3], up[2], up[1]])

    def block(z):
        index = jnp.bitwise_and(z - place, 7).astype(jnp.uint32)
        return lax.dynamic_index_in_dim(ring, index, 0, keepdims=False)

    return ring, block


def modulate(level, w_mod, core):
    width = w_mod.shape[1] // 12
    depth = w_mod.shape[0]

    def body(core_ref, level_ref, w_ref, out_ref):
        out_ref[...] = jnp.dot(level_ref[...], w_ref[...], preferred_element_type=F32)

    return pl.pallas_call(
        body,
        grid_spec=pltpu.PrefetchScalarGridSpec(
            num_scalar_prefetch=1,
            grid=(6,),
            in_specs=[
                pl.BlockSpec((16, depth), lambda j, core_ref: (0, 0)),
                pl.BlockSpec(
                    (depth, width), lambda j, core_ref: (0, (j // 2) * 4 + (j % 2) * 2 + core_ref[0])
                ),
            ],
            out_specs=pl.BlockSpec((16, width), lambda j, core_ref: (0, j)),
        ),
        out_shape=jax.ShapeDtypeStruct((16, 6 * width), F32),
        cost_estimate=pl.CostEstimate(
            flops=2 * 16 * depth * 6 * width, bytes_accessed=2 * depth * 6 * width, transcendentals=0
        ),
        name="modulate",
    )(core.reshape(1).astype(jnp.int32), jnp.broadcast_to(level, (16, depth)), w_mod)[0]


def sum_depth(down_blocks, up_blocks, extra, place):
    half = down_blocks.shape[1]

    def block(offset):
        index = jnp.bitwise_and(place + offset, 7).astype(jnp.uint32)
        pair = [
            lax.dynamic_index_in_dim(blocks, index, 0, keepdims=False)
            for blocks in (down_blocks, up_blocks)
        ]
        return jnp.concatenate(pair + [extra])

    def add(a, b):
        return (a.astype(F32) + b.astype(F32)).astype(BF16)

    far = block(4)
    up = shift_by(far[:half], DEPTH, 1)
    down = shift_by(far[half:], DEPTH, -1)
    mine = block(3)
    up = jnp.concatenate([add(mine[:half], up), mine[half:]])
    mine = block(-3)
    down = jnp.concatenate([mine[:half], add(mine[half:], down)])
    up = shift_by(up, DEPTH, 1)
    down = shift_by(down, DEPTH, -1)
    for offset in (2, 1):
        up = shift_by(add(block(offset), up), DEPTH, 1)
        down = shift_by(add(block(-offset), down), DEPTH, -1)
    return finish(block(0), up, down)


def dot(a, b, ca, cb):
    return lax.dot_general(a, b, (((ca,), (cb,)), ((), ())), preferred_element_type=F32)


def per_device(tokens, target, step_index, plan, w_mod, w_up, w_down):
    z_half = lax.axis_index("zh")
    core = lax.axis_index("core")
    place = lax.axis_index(DEPTH)
    group = lax.axis_index(PLANE)
    width = tokens.shape[1]
    rows = tokens.shape[0] // 2
    full_width = 4 * width
    token_count = tokens.shape[0] * 64
    piece = w_down.shape[0] // 16

    def by_core(own, other):
        return jnp.where(core == 0, own, other), jnp.where(core == 0, other, own)

    up_part = lax.dynamic_slice_in_dim(w_up, group * piece, piece, 1).T
    down_part = lax.dynamic_slice_in_dim(w_down, group * piece, piece, 0)
    both = jnp.stack([tokens.reshape(2, rows, width), target.reshape(2, rows, width)], axis=1)
    own = lax.dynamic_index_in_dim(both, z_half, 0, keepdims=False)
    other = shift_by(lax.dynamic_index_in_dim(both, 1 - z_half, 0, keepdims=False), "zh", 1)
    other, part = lax.optimization_barrier((other, jnp.concatenate([up_part, down_part])))
    joined = jnp.where(
        z_half == 0, jnp.concatenate([own, other], axis=2), jnp.concatenate([other, own], axis=2)
    ).astype(F32)
    values, goal = joined[0], joined[1]

    picked = jnp.where(jnp.arange(plan.shape[0]) == step_index[0], plan, 0)
    time_value = jnp.sum(picked).astype(F32)
    half_width = w_mod.shape[0] // 2
    frequency = jnp.exp(-math.log(10000.0) * jnp.arange(half_width, dtype=F32) / half_width)
    angles = time_value * frequency
    embed = jnp.concatenate([jnp.cos(angles), jnp.sin(angles)])
    mod = modulate(jax.nn.silu(embed).astype(BF16), w_mod, core)
    ring, weights = gather_depth(part, place)
    down = jnp.concatenate(
        [jnp.concatenate([weights(4 * h + c)[piece:] for c in range(4)]) for h in (0, 1)], axis=1
    )
    kept, given = split_ring(ring, place, core)
    up = join_cores(kept, shift_by(given, "core", 1), core)
    shift, scale, gate = mod.reshape(3, 2 * width)

    local_mean = jnp.mean(values, axis=1)
    local_dev = jnp.sum(jnp.square(values - local_mean[:, None]), axis=1)
    far_mean, far_dev = shift_by(jnp.stack([local_mean, local_dev]), "core", 1)
    average = 0.5 * (local_mean + far_mean)
    spread = (
        local_dev + far_dev + jnp.square(local_mean - far_mean) * (0.5 * width * 2)
    ) / full_width
    normed = (
        (values - average[:, None]) * lax.rsqrt(spread + 1e-06)[:, None] * (1.0 + scale) + shift
    ).astype(BF16)

    normed_all = gather_plane(normed).reshape(16 * rows, 2 * width)
    hidden = dot(normed_all, up, 1, 1).astype(BF16)
    activ, slope = activate(hidden, shift_by(hidden, "core", 1))
    line = activ.reshape(4, 4 * rows, 4 * piece)
    mixed = {s: dot(line[s], down, 1, 0).astype(BF16) for s in (1, 3, 2, 0)}
    mixed = sum_line(mixed, True).astype(BF16)
    mixed = sum_line(mixed.reshape(4, rows, 2 * width), False)
    residual = values + gate * mixed - goal
    squares = jnp.broadcast_to(jnp.sum(residual * residual, keepdims=True), (8, 128))
    extra = encode(squares, shift_by(squares, "core", 1), place, width)
    delta = (gate * residual * (1.0 / math.sqrt(token_count))).astype(BF16)

    delta_all = gather_plane(delta).reshape(16 * rows, 2 * width)
    delta_all, extra = lax.optimization_barrier((delta_all, extra))
    hidden_grad = dot(delta_all, down, 1, 1).astype(BF16)
    far = shift_by(hidden_grad, "core", 1)
    down_blocks = [
        dot(activ, delta_all[:, h * width : (h + 1) * width], 0, 0).astype(BF16) for h in (0, 1)
    ]
    down_blocks = jnp.concatenate(down_blocks).reshape(8, piece, width)
    delta_hidden = slope_grad(hidden_grad, far, slope)
    up_grad = jnp.stack(
        [dot(delta_hidden, normed_all[:, h * width : (h + 1) * width], 0, 0).astype(BF16) for h in (0, 1)]
    ).reshape(2, 2, 2, piece, width)
    kept = lax.dynamic_index_in_dim(up_grad, core, 2, keepdims=False)
    given = shift_by(lax.dynamic_index_in_dim(up_grad, 1 - core, 2, keepdims=False), "core", 1)
    pair = by_core(kept, given)
    up_blocks = jnp.stack(pair, axis=2)
    up_blocks = jnp.swapaxes(up_blocks, 0, 1).reshape(8, piece, width)

    grad_down, grad_up = sum_depth(down_blocks, up_blocks, extra, place)
    share = width // 16
    grad_up = lax.all_to_all(grad_up, PLANE, split_axis=0, concat_axis=0, tiled=True)
    mean_loss = jnp.sum(grad_up[:, share, :3].astype(F32)) / (token_count * full_width)
    grad_up = jnp.swapaxes(grad_up[:, :share], 0, 1).reshape(share, -1)
    return mean_loss, grad_up, grad_down


def solution(mesh):
    fine = Mesh(mesh.devices.reshape([SIZES[name] for name in AXES]), AXES)
    token_spec = P(("y", "x", "zl"), ("zh", "core"))
    weight_spec = P("zl", ("zh", "core"))
    grad_spec = P(("zl", "y", "x"), ("zh", "core"))
    return jax.shard_map(
        per_device,
        mesh=fine,
        in_specs=(token_spec, token_spec, P(PLANE), P(), P(), weight_spec, weight_spec),
        out_specs=(P(), grad_spec, grad_spec),
        check_vma=False,
    )
```

```python
import math

import jax
import jax.numpy as jnp
from jax import lax
from jax.experimental import pallas as pl
from jax.experimental.pallas import tpu as pltpu
from jax.sharding import Mesh, PartitionSpec as P

GELU_COEF = math.sqrt(2.0 / math.pi)
CUBIC_COEF = 0.044715
AXES = ("y", "x", "zh", "core", "zl")
SIZES = dict(zip(AXES, (4, 4, 2, 2, 4)))
PLANE = ("y", "x")
DEPTH = ("zh", "zl")
F32 = jnp.float32
BF16 = jnp.bfloat16


def shift_by(value, axis, offset):
    names = (axis,) if isinstance(axis, str) else axis
    count = math.prod(SIZES[name] for name in names)
    return lax.ppermute(value, axis, [(i, (i + offset) % count) for i in range(count)])


def turn_by(value, offset, turn):
    ny, nx = SIZES["y"], SIZES["x"]

    def index(y, x, core):
        return ((y % ny) * nx + x % nx) * 2 + core

    pairs = []
    for y in range(ny):
        for x in range(nx):
            for core in range(2):
                along_x = (core == 0) != turn
                goal = index(y, x + offset, core) if along_x else index(y + offset, x, core)
                pairs.append((index(y, x, core), goal))
    return lax.ppermute(value, ("y", "x", "core"), pairs)


def gather_line(value, turn):
    one, three, two = (turn_by(value, s, turn) for s in (1, 3, 2))
    return jnp.stack([value, one, two, three])


def gather_plane(value):
    return gather_line(gather_line(value, False), True)


def sum_line(blocks, turn):
    parts = [turn_by(blocks[s], -s, turn) for s in (1, 3, 2)]
    return blocks[0].astype(F32) + parts[0].astype(F32) + parts[1].astype(F32) + parts[2].astype(F32)


def local_call(body, outs, *operands, name, cost):
    specs = [
        pl.BlockSpec(memory_space=pltpu.SMEM if value.ndim == 1 else pltpu.VMEM) for value in operands
    ]
    size = sum(value.size * value.dtype.itemsize for value in list(operands) + outs)
    return pl.pallas_call(
        body,
        in_specs=specs,
        out_specs=[pl.BlockSpec(memory_space=pltpu.VMEM)] * len(outs),
        out_shape=outs,
        cost_estimate=pl.CostEstimate(flops=cost, bytes_accessed=size, transcendentals=0),
        compiler_params=pltpu.CompilerParams(vmem_limit_bytes=2 * size + (8 << 20)),
        name=name,
    )(*operands)


def pair_blocks(count):
    step = count // 16
    for i in range(16):
        j = (i % 4) * 4 + i // 4
        yield slice(i * step, (i + 1) * step), slice(j * step, (j + 1) * step)


def activate(own, far):
    def body(own_ref, far_ref, activ_ref, slope_ref):
        for here, there in pair_blocks(own.shape[0]):
            hidden = own_ref[here].astype(F32) + far_ref[there].astype(F32)
            square = hidden * hidden
            tanh_value = jnp.tanh(GELU_COEF * (hidden + CUBIC_COEF * square * hidden))
            half = 0.5 * (1.0 + tanh_value)
            activ_ref[here] = (hidden * half).astype(BF16)
            slope_ref[here] = half + 0.5 * hidden * (1.0 - tanh_value * tanh_value) * GELU_COEF * (
                1.0 + 3.0 * CUBIC_COEF * square
            )

    outs = [jax.ShapeDtypeStruct(own.shape, BF16), jax.ShapeDtypeStruct(own.shape, F32)]
    return local_call(body, outs, own, far, name="activate", cost=20 * own.size)


def slope_grad(own, far, slope):
    def body(own_ref, far_ref, slope_ref, out_ref):
        for here, there in pair_blocks(own.shape[0]):
            total = own_ref[here].astype(F32) + far_ref[there].astype(F32)
            out_ref[here] = (total * slope_ref[here]).astype(BF16)

    outs = [jax.ShapeDtypeStruct(own.shape, BF16)]
    return local_call(body, outs, own, far, slope, name="slope_grad", cost=3 * own.size)[0]


def split_ring(ring, place, core):
    rows, width = ring.shape[1] // 2, ring.shape[2]

    def body(index_ref, ring_ref, kept_ref, given_ref):
        for h in (0, 1):
            for c in (0, 1):
                first = 4 * h + 2 * c - index_ref[0]
                kept_ref[h, c] = ring_ref[jnp.bitwise_and(first + index_ref[1], 7), 0:rows]
                given_ref[h, c] = ring_ref[jnp.bitwise_and(first + 1 - index_ref[1], 7), 0:rows]

    outs = [jax.ShapeDtypeStruct((2, 2, rows, width), BF16)] * 2
    index = jnp.stack([place, core]).astype(jnp.int32)
    return local_call(body, outs, index, ring, name="split_ring", cost=8 * rows * width)


def join_cores(kept, given, core):
    rows, width = kept.shape[2:]

    def body(core_ref, kept_ref, given_ref, out_ref):
        for h in (0, 1):
            for c in (0, 1):
                own = pl.multiple_of((2 * h + core_ref[0]) * rows, 16)
                far = pl.multiple_of((2 * h + 1 - core_ref[0]) * rows, 16)
                columns = slice(c * width, (c + 1) * width)
                out_ref[pl.ds(own, rows), columns] = kept_ref[h, c]
                out_ref[pl.ds(far, rows), columns] = given_ref[h, c]

    outs = [jax.ShapeDtypeStruct((4 * rows, 2 * width), BF16)]
    index = core.reshape(1).astype(jnp.int32)
    return local_call(body, outs, index, kept, given, name="join_cores", cost=8 * rows * width)[0]


def triple(value, lane):
    high = value.astype(BF16).astype(F32)
    middle = (value - high).astype(BF16).astype(F32)
    low = value - high - middle
    terms = jnp.where(lane == 0, high, jnp.where(lane == 1, middle, low))
    return jnp.where((lane >= 0) & (lane < 3), terms, 0.0).astype(BF16)


def encode(own, far, place, width):
    def body(place_ref, own_ref, far_ref, out_ref):
        value = jnp.broadcast_to(own_ref[0:1, 0:1] + far_ref[0:1, 0:1], (16, width))
        lane = lax.broadcasted_iota(jnp.int32, (16, width), 1) - 3 * place_ref[0]
        out_ref[...] = triple(value, lane)

    return pl.pallas_call(
        body,
        in_specs=[pl.BlockSpec(memory_space=pltpu.SMEM)] + [pl.BlockSpec(memory_space=pltpu.VMEM)] * 2,
        out_specs=pl.BlockSpec(memory_space=pltpu.VMEM),
        out_shape=jax.ShapeDtypeStruct((16, width), BF16),
        cost_estimate=pl.CostEstimate(flops=16 * width, bytes_accessed=48 * width, transcendentals=0),
        name="encode",
    )(place.reshape(1).astype(jnp.int32), own, far)


def finish(own, up, down):
    piece = (own.shape[0] - 16) // 2
    width = own.shape[1]
    share = width // 16

    def body(own_ref, up_ref, down_ref, grad_ref, send_ref):
        def total(first, last):
            return (
                own_ref[first:last].astype(F32)
                + up_ref[first:last].astype(F32)
                + down_ref[first:last].astype(F32)
            )

        grad_ref[...] = total(0, piece).astype(BF16)
        turned = total(piece, 2 * piece).T.astype(BF16)
        squares = jnp.sum(total(2 * piece, 2 * piece + 16)[0:1], axis=1, keepdims=True)
        lane = lax.broadcasted_iota(jnp.int32, (16, piece), 1)
        note = triple(jnp.broadcast_to(squares, (16, piece)), lane)
        for p in range(16):
            send_ref[p, 0:share] = turned[p * share : (p + 1) * share]
            send_ref[p, share : share + 16] = note

    return pl.pallas_call(
        body,
        in_specs=[pl.BlockSpec(memory_space=pltpu.VMEM)] * 3,
        out_specs=[pl.BlockSpec(memory_space=pltpu.VMEM)] * 2,
        out_shape=[
            jax.ShapeDtypeStruct((piece, width), BF16),
            jax.ShapeDtypeStruct((16, share + 16, piece), BF16),
        ],
        cost_estimate=pl.CostEstimate(
            flops=4 * own.size, bytes_accessed=10 * own.size, transcendentals=0
        ),
        name="finish",
    )(own, up, down)


def gather_depth(value, place):
    half = value.shape[0] // 2
    up, down = [value], [value]
    for _ in range(3):
        up.append(shift_by(up[-1], DEPTH, 1))
        down.append(shift_by(down[-1], DEPTH, -1))
    far = [shift_by(up[-1][:half], DEPTH, 1), shift_by(down[-1][half:], DEPTH, -1)]
    ring = jnp.stack([value, down[1], down[2], down[3], jnp.concatenate(far), up[3], up[2], up[1]])

    def block(z):
        index = jnp.bitwise_and(z - place, 7).astype(jnp.uint32)
        return lax.dynamic_index_in_dim(ring, index, 0, keepdims=False)

    return ring, block


def modulate(level, w_mod, core):
    width = w_mod.shape[1] // 12
    depth = w_mod.shape[0]

    def body(core_ref, level_ref, *refs):
        for j in range(6):
            terms = level_ref[...] * refs[j][...].astype(F32)
            refs[6][0:1, j * width : (j + 1) * width] = jnp.sum(terms, axis=0, keepdims=True)

    def block(j):
        first = (j // 2) * 4 + (j % 2) * 2
        return pl.BlockSpec((depth, width), lambda i, core_ref: (0, first + core_ref[0]))

    return pl.pallas_call(
        body,
        grid_spec=pltpu.PrefetchScalarGridSpec(
            num_scalar_prefetch=1,
            grid=(1,),
            in_specs=[pl.BlockSpec((depth, 1), lambda i, core_ref: (0, 0))]
            + [block(j) for j in range(6)],
            out_specs=pl.BlockSpec((8, 6 * width), lambda i, core_ref: (0, 0)),
        ),
        out_shape=jax.ShapeDtypeStruct((8, 6 * width), F32),
        cost_estimate=pl.CostEstimate(
            flops=12 * depth * width, bytes_accessed=12 * depth * width, transcendentals=0
        ),
        compiler_params=pltpu.CompilerParams(vmem_limit_bytes=16 << 20),
        name="modulate",
    )(core.reshape(1).astype(jnp.int32), level, *([w_mod] * 6))[0]


def unpack(parts, factor):
    count, rows, piece = parts.shape
    share = rows - 16

    def body(part_ref, grad_ref, loss_ref):
        total = part_ref[0, share : share + 16].astype(F32)
        for p in range(1, count):
            total += part_ref[p, share : share + 16].astype(F32)
        loss_ref[...] = jnp.broadcast_to(
            jnp.sum(total[0:1], axis=1, keepdims=True) * factor, loss_ref.shape
        )
        for p in range(count):
            grad_ref[:, p * piece : (p + 1) * piece] = part_ref[p, 0:share]

    outs = [
        jax.ShapeDtypeStruct((share, count * piece), BF16),
        jax.ShapeDtypeStruct((8, 128), F32),
    ]
    return local_call(body, outs, parts, name="unpack", cost=parts.size)


def sum_depth(down_blocks, up_blocks, extra, place):
    half = down_blocks.shape[1]

    def block(offset):
        index = jnp.bitwise_and(place + offset, 7).astype(jnp.uint32)
        pair = [
            lax.dynamic_index_in_dim(blocks, index, 0, keepdims=False)
            for blocks in (down_blocks, up_blocks)
        ]
        return jnp.concatenate(pair + [extra])

    def add(a, b):
        return (a.astype(F32) + b.astype(F32)).astype(BF16)

    far = block(4)
    up = shift_by(far[:half], DEPTH, 1)
    down = shift_by(far[half:], DEPTH, -1)
    mine = block(3)
    up = jnp.concatenate([add(mine[:half], up), mine[half:]])
    mine = block(-3)
    down = jnp.concatenate([mine[:half], add(mine[half:], down)])
    up = shift_by(up, DEPTH, 1)
    down = shift_by(down, DEPTH, -1)
    for offset in (2, 1):
        up = shift_by(add(block(offset), up), DEPTH, 1)
        down = shift_by(add(block(-offset), down), DEPTH, -1)
    return finish(block(0), up, down)


def dot(a, b, ca, cb):
    return lax.dot_general(a, b, (((ca,), (cb,)), ((), ())), preferred_element_type=F32)


def per_device(tokens, target, step_index, plan, w_mod, w_up, w_down):
    z_half = lax.axis_index("zh")
    core = lax.axis_index("core")
    place = lax.axis_index(DEPTH)
    group = lax.axis_index(PLANE)
    width = tokens.shape[1]
    rows = tokens.shape[0] // 2
    full_width = 4 * width
    token_count = tokens.shape[0] * 64
    piece = w_down.shape[0] // 16

    def by_core(own, other):
        return jnp.where(core == 0, own, other), jnp.where(core == 0, other, own)

    up_part = lax.dynamic_slice_in_dim(w_up, group * piece, piece, 1).T
    down_part = lax.dynamic_slice_in_dim(w_down, group * piece, piece, 0)
    both = jnp.stack([tokens.reshape(2, rows, width), target.reshape(2, rows, width)], axis=1)
    own = lax.dynamic_index_in_dim(both, z_half, 0, keepdims=False)
    other = shift_by(lax.dynamic_index_in_dim(both, 1 - z_half, 0, keepdims=False), "zh", 1)
    other, part = lax.optimization_barrier((other, jnp.concatenate([up_part, down_part])))
    joined = jnp.where(
        z_half == 0, jnp.concatenate([own, other], axis=2), jnp.concatenate([other, own], axis=2)
    ).astype(F32)
    values, goal = joined[0], joined[1]

    picked = jnp.where(jnp.arange(plan.shape[0]) == step_index[0], plan, 0)
    time_value = jnp.sum(picked).astype(F32)
    half_width = w_mod.shape[0] // 2
    frequency = jnp.exp(-math.log(10000.0) * jnp.arange(half_width, dtype=F32) / half_width)
    angles = time_value * frequency
    embed = jnp.concatenate([jnp.cos(angles), jnp.sin(angles)])
    level = jax.nn.silu(embed).astype(BF16).astype(F32)[:, None]
    mod = modulate(level, w_mod, core)
    ring, weights = gather_depth(part, place)
    down = jnp.concatenate(
        [jnp.concatenate([weights(4 * h + c)[piece:] for c in range(4)]) for h in (0, 1)], axis=1
    )
    kept, given = split_ring(ring, place, core)
    up = join_cores(kept, shift_by(given, "core", 1), core)
    shift, scale, gate = mod.reshape(3, 2 * width)

    local_mean = jnp.mean(values, axis=1)
    local_dev = jnp.sum(jnp.square(values - local_mean[:, None]), axis=1)
    far_mean, far_dev = shift_by(jnp.stack([local_mean, local_dev]), "core", 1)
    average = 0.5 * (local_mean + far_mean)
    spread = (
        local_dev + far_dev + jnp.square(local_mean - far_mean) * (0.5 * width * 2)
    ) / full_width
    normed = (
        (values - average[:, None]) * lax.rsqrt(spread + 1e-06)[:, None] * (1.0 + scale) + shift
    ).astype(BF16)

    normed_all = gather_plane(normed).reshape(16 * rows, 2 * width)
    hidden = dot(normed_all, up, 1, 1).astype(BF16)
    activ, slope = activate(hidden, shift_by(hidden, "core", 1))
    line = activ.reshape(4, 4 * rows, 4 * piece)
    mixed = {s: dot(line[s], down, 1, 0).astype(BF16) for s in (1, 3, 2, 0)}
    mixed = sum_line(mixed, True).astype(BF16)
    mixed = sum_line(mixed.reshape(4, rows, 2 * width), False)
    residual = values + gate * mixed - goal
    squares = jnp.broadcast_to(jnp.sum(residual * residual, keepdims=True), (8, 128))
    extra = encode(squares, shift_by(squares, "core", 1), place, width)
    delta = (gate * residual * (1.0 / math.sqrt(token_count))).astype(BF16)

    delta_all = gather_plane(delta).reshape(16 * rows, 2 * width)
    delta_all, extra = lax.optimization_barrier((delta_all, extra))
    hidden_grad = dot(delta_all, down, 1, 1).astype(BF16)
    far = shift_by(hidden_grad, "core", 1)
    down_blocks = [
        dot(activ, delta_all[:, h * width : (h + 1) * width], 0, 0).astype(BF16) for h in (0, 1)
    ]
    down_blocks = jnp.concatenate(down_blocks).reshape(8, piece, width)
    delta_hidden = slope_grad(hidden_grad, far, slope)
    up_grad = jnp.stack(
        [dot(delta_hidden, normed_all[:, h * width : (h + 1) * width], 0, 0).astype(BF16) for h in (0, 1)]
    ).reshape(2, 2, 2, piece, width)
    kept = lax.dynamic_index_in_dim(up_grad, core, 2, keepdims=False)
    given = shift_by(lax.dynamic_index_in_dim(up_grad, 1 - core, 2, keepdims=False), "core", 1)
    pair = by_core(kept, given)
    up_blocks = jnp.stack(pair, axis=2)
    up_blocks = jnp.swapaxes(up_blocks, 0, 1).reshape(8, piece, width)

    grad_down, grad_up = sum_depth(down_blocks, up_blocks, extra, place)
    grad_up = lax.all_to_all(grad_up, PLANE, split_axis=0, concat_axis=0, tiled=True)
    grad_up, loss = unpack(grad_up, 1.0 / (token_count * full_width))
    mean_loss = loss[0, 0]
    return mean_loss, grad_up, grad_down


def solution(mesh):
    fine = Mesh(mesh.devices.reshape([SIZES[name] for name in AXES]), AXES)
    token_spec = P(("y", "x", "zl"), ("zh", "core"))
    weight_spec = P("zl", ("zh", "core"))
    grad_spec = P(("zl", "y", "x"), ("zh", "core"))
    return jax.shard_map(
        per_device,
        mesh=fine,
        in_specs=(token_spec, token_spec, P(PLANE), P(), P(), weight_spec, weight_spec),
        out_specs=(P(), grad_spec, grad_spec),
        check_vma=False,
    )
```

```python
import math

import jax
import jax.numpy as jnp
from jax import lax
from jax.experimental import pallas as pl
from jax.experimental.pallas import tpu as pltpu
from jax.sharding import Mesh, PartitionSpec as P

GELU_COEF = math.sqrt(2.0 / math.pi)
CUBIC_COEF = 0.044715
AXES = ("y", "x", "zh", "core", "zl")
SIZES = dict(zip(AXES, (4, 4, 2, 2, 4)))
PLANE = ("y", "x")
DEPTH = ("zh", "zl")
F32 = jnp.float32
BF16 = jnp.bfloat16


def shift_by(value, axis, offset):
    names = (axis,) if isinstance(axis, str) else axis
    count = math.prod(SIZES[name] for name in names)
    return lax.ppermute(value, axis, [(i, (i + offset) % count) for i in range(count)])


def turn_by(value, offset, turn):
    ny, nx = SIZES["y"], SIZES["x"]

    def index(y, x, core):
        return ((y % ny) * nx + x % nx) * 2 + core

    pairs = []
    for y in range(ny):
        for x in range(nx):
            for core in range(2):
                along_x = (core == 0) != turn
                goal = index(y, x + offset, core) if along_x else index(y + offset, x, core)
                pairs.append((index(y, x, core), goal))
    return lax.ppermute(value, ("y", "x", "core"), pairs)


def gather_line(value, turn):
    one, three, two = (turn_by(value, s, turn) for s in (1, 3, 2))
    return jnp.stack([value, one, two, three])


def gather_plane(value):
    return gather_line(gather_line(value, False), True)


def sum_line(blocks, turn):
    parts = [turn_by(blocks[s], -s, turn) for s in (1, 3, 2)]
    return blocks[0].astype(F32) + parts[0].astype(F32) + parts[1].astype(F32) + parts[2].astype(F32)


def local_call(body, outs, *operands, name, cost):
    specs = [
        pl.BlockSpec(memory_space=pltpu.SMEM if value.ndim == 1 else pltpu.VMEM) for value in operands
    ]
    size = sum(value.size * value.dtype.itemsize for value in list(operands) + outs)
    return pl.pallas_call(
        body,
        in_specs=specs,
        out_specs=[pl.BlockSpec(memory_space=pltpu.VMEM)] * len(outs),
        out_shape=outs,
        cost_estimate=pl.CostEstimate(flops=cost, bytes_accessed=size, transcendentals=0),
        compiler_params=pltpu.CompilerParams(vmem_limit_bytes=2 * size + (8 << 20)),
        name=name,
    )(*operands)


def pair_blocks(count):
    step = count // 16
    for i in range(16):
        j = (i % 4) * 4 + i // 4
        yield slice(i * step, (i + 1) * step), slice(j * step, (j + 1) * step)


def bend(hidden):
    return jnp.tanh(GELU_COEF * (hidden + CUBIC_COEF * hidden * hidden * hidden))


def activate(own, far):
    def body(own_ref, far_ref, activ_ref):
        for here, there in pair_blocks(own.shape[0]):
            hidden = own_ref[here].astype(F32) + far_ref[there].astype(F32)
            activ_ref[here] = (0.5 * hidden * (1.0 + bend(hidden))).astype(BF16)

    outs = [jax.ShapeDtypeStruct(own.shape, BF16)]
    return local_call(body, outs, own, far, name="activate", cost=10 * own.size)[0]


def gelu_slope(own, far):
    def body(own_ref, far_ref, slope_ref):
        for here, there in pair_blocks(own.shape[0]):
            hidden = own_ref[here].astype(F32) + far_ref[there].astype(F32)
            tanh_value = bend(hidden)
            slope_ref[here] = 0.5 * (1.0 + tanh_value) + 0.5 * hidden * (
                1.0 - tanh_value * tanh_value
            ) * GELU_COEF * (1.0 + 3.0 * CUBIC_COEF * hidden * hidden)

    outs = [jax.ShapeDtypeStruct(own.shape, F32)]
    return local_call(body, outs, own, far, name="gelu_slope", cost=20 * own.size)[0]


def slope_grad(own, far, slope):
    def body(own_ref, far_ref, slope_ref, out_ref):
        for here, there in pair_blocks(own.shape[0]):
            total = own_ref[here].astype(F32) + far_ref[there].astype(F32)
            out_ref[here] = (total * slope_ref[here]).astype(BF16)

    outs = [jax.ShapeDtypeStruct(own.shape, BF16)]
    return local_call(body, outs, own, far, slope, name="slope_grad", cost=3 * own.size)[0]


def split_ring(ring, place, core):
    rows, width = ring.shape[1] // 2, ring.shape[2]

    def body(index_ref, ring_ref, kept_ref, given_ref):
        for h in (0, 1):
            for c in (0, 1):
                first = 4 * h + 2 * c - index_ref[0]
                kept_ref[h, c] = ring_ref[jnp.bitwise_and(first + index_ref[1], 7), 0:rows]
                given_ref[h, c] = ring_ref[jnp.bitwise_and(first + 1 - index_ref[1], 7), 0:rows]

    outs = [jax.ShapeDtypeStruct((2, 2, rows, width), BF16)] * 2
    index = jnp.stack([place, core]).astype(jnp.int32)
    return local_call(body, outs, index, ring, name="split_ring", cost=8 * rows * width)


def join_cores(kept, given, core):
    rows, width = kept.shape[2:]

    def body(core_ref, kept_ref, given_ref, out_ref):
        for h in (0, 1):
            for c in (0, 1):
                own = pl.multiple_of((2 * h + core_ref[0]) * rows, 16)
                far = pl.multiple_of((2 * h + 1 - core_ref[0]) * rows, 16)
                columns = slice(c * width, (c + 1) * width)
                out_ref[pl.ds(own, rows), columns] = kept_ref[h, c]
                out_ref[pl.ds(far, rows), columns] = given_ref[h, c]

    outs = [jax.ShapeDtypeStruct((4 * rows, 2 * width), BF16)]
    index = core.reshape(1).astype(jnp.int32)
    return local_call(body, outs, index, kept, given, name="join_cores", cost=8 * rows * width)[0]


def triple(value, lane):
    high = value.astype(BF16).astype(F32)
    middle = (value - high).astype(BF16).astype(F32)
    low = value - high - middle
    terms = jnp.where(lane == 0, high, jnp.where(lane == 1, middle, low))
    return jnp.where((lane >= 0) & (lane < 3), terms, 0.0).astype(BF16)


def encode(own, far, place, width):
    def body(place_ref, own_ref, far_ref, out_ref):
        value = jnp.broadcast_to(own_ref[0:1, 0:1] + far_ref[0:1, 0:1], (16, width))
        lane = lax.broadcasted_iota(jnp.int32, (16, width), 1) - 3 * place_ref[0]
        out_ref[...] = triple(value, lane)

    return pl.pallas_call(
        body,
        in_specs=[pl.BlockSpec(memory_space=pltpu.SMEM)] + [pl.BlockSpec(memory_space=pltpu.VMEM)] * 2,
        out_specs=pl.BlockSpec(memory_space=pltpu.VMEM),
        out_shape=jax.ShapeDtypeStruct((16, width), BF16),
        cost_estimate=pl.CostEstimate(flops=16 * width, bytes_accessed=48 * width, transcendentals=0),
        name="encode",
    )(place.reshape(1).astype(jnp.int32), own, far)


def finish(own, up, down):
    piece = (own.shape[0] - 16) // 2
    width = own.shape[1]
    share = width // 16

    def body(own_ref, up_ref, down_ref, grad_ref, send_ref):
        def total(first, last):
            return (
                own_ref[first:last].astype(F32)
                + up_ref[first:last].astype(F32)
                + down_ref[first:last].astype(F32)
            )

        grad_ref[...] = total(0, piece).astype(BF16)
        turned = total(piece, 2 * piece).T.astype(BF16)
        squares = jnp.sum(total(2 * piece, 2 * piece + 16)[0:1], axis=1, keepdims=True)
        lane = lax.broadcasted_iota(jnp.int32, (16, piece), 1)
        note = triple(jnp.broadcast_to(squares, (16, piece)), lane)
        for p in range(16):
            send_ref[p, 0:share] = turned[p * share : (p + 1) * share]
            send_ref[p, share : share + 16] = note

    return pl.pallas_call(
        body,
        in_specs=[pl.BlockSpec(memory_space=pltpu.VMEM)] * 3,
        out_specs=[pl.BlockSpec(memory_space=pltpu.VMEM)] * 2,
        out_shape=[
            jax.ShapeDtypeStruct((piece, width), BF16),
            jax.ShapeDtypeStruct((16, share + 16, piece), BF16),
        ],
        cost_estimate=pl.CostEstimate(
            flops=4 * own.size, bytes_accessed=10 * own.size, transcendentals=0
        ),
        name="finish",
    )(own, up, down)


def gather_depth(value, place):
    half = value.shape[0] // 2
    up, down = [value], [value]
    for _ in range(3):
        up.append(shift_by(up[-1], DEPTH, 1))
        down.append(shift_by(down[-1], DEPTH, -1))
    far = [shift_by(up[-1][:half], DEPTH, 1), shift_by(down[-1][half:], DEPTH, -1)]
    ring = jnp.stack([value, down[1], down[2], down[3], jnp.concatenate(far), up[3], up[2], up[1]])

    def block(z):
        index = jnp.bitwise_and(z - place, 7).astype(jnp.uint32)
        return lax.dynamic_index_in_dim(ring, index, 0, keepdims=False)

    return ring, block


def modulate(level, w_mod, core):
    width = w_mod.shape[1] // 12
    depth = w_mod.shape[0]

    def body(core_ref, level_ref, *refs):
        for j in range(6):
            terms = level_ref[...] * refs[j][...].astype(F32)
            refs[6][0:1, j * width : (j + 1) * width] = jnp.sum(terms, axis=0, keepdims=True)

    def block(j):
        first = (j // 2) * 4 + (j % 2) * 2
        return pl.BlockSpec((depth, width), lambda i, core_ref: (0, first + core_ref[0]))

    return pl.pallas_call(
        body,
        grid_spec=pltpu.PrefetchScalarGridSpec(
            num_scalar_prefetch=1,
            grid=(1,),
            in_specs=[pl.BlockSpec((depth, 1), lambda i, core_ref: (0, 0))]
            + [block(j) for j in range(6)],
            out_specs=pl.BlockSpec((8, 6 * width), lambda i, core_ref: (0, 0)),
        ),
        out_shape=jax.ShapeDtypeStruct((8, 6 * width), F32),
        cost_estimate=pl.CostEstimate(
            flops=12 * depth * width, bytes_accessed=12 * depth * width, transcendentals=0
        ),
        compiler_params=pltpu.CompilerParams(vmem_limit_bytes=16 << 20),
        name="modulate",
    )(core.reshape(1).astype(jnp.int32), level, *([w_mod] * 6))[0]


def unpack(parts, factor):
    count, rows, piece = parts.shape
    share = rows - 16

    def body(part_ref, grad_ref, loss_ref):
        total = part_ref[0, share : share + 16].astype(F32)
        for p in range(1, count):
            total += part_ref[p, share : share + 16].astype(F32)
        loss_ref[...] = jnp.broadcast_to(
            jnp.sum(total[0:1], axis=1, keepdims=True) * factor, loss_ref.shape
        )
        for p in range(count):
            grad_ref[:, p * piece : (p + 1) * piece] = part_ref[p, 0:share]

    outs = [
        jax.ShapeDtypeStruct((share, count * piece), BF16),
        jax.ShapeDtypeStruct((8, 128), F32),
    ]
    return local_call(body, outs, parts, name="unpack", cost=parts.size)


def sum_depth(down_blocks, up_blocks, extra, place):
    half = down_blocks.shape[1]

    def block(offset):
        index = jnp.bitwise_and(place + offset, 7).astype(jnp.uint32)
        pair = [
            lax.dynamic_index_in_dim(blocks, index, 0, keepdims=False)
            for blocks in (down_blocks, up_blocks)
        ]
        return jnp.concatenate(pair + [extra])

    def add(a, b):
        return (a.astype(F32) + b.astype(F32)).astype(BF16)

    far = block(4)
    up = shift_by(far[:half], DEPTH, 1)
    down = shift_by(far[half:], DEPTH, -1)
    mine = block(3)
    up = jnp.concatenate([add(mine[:half], up), mine[half:]])
    mine = block(-3)
    down = jnp.concatenate([mine[:half], add(mine[half:], down)])
    up = shift_by(up, DEPTH, 1)
    down = shift_by(down, DEPTH, -1)
    for offset in (2, 1):
        up = shift_by(add(block(offset), up), DEPTH, 1)
        down = shift_by(add(block(-offset), down), DEPTH, -1)
    return finish(block(0), up, down)


def dot(a, b, ca, cb):
    return lax.dot_general(a, b, (((ca,), (cb,)), ((), ())), preferred_element_type=F32)


def per_device(tokens, target, step_index, plan, w_mod, w_up, w_down):
    z_half = lax.axis_index("zh")
    core = lax.axis_index("core")
    place = lax.axis_index(DEPTH)
    group = lax.axis_index(PLANE)
    width = tokens.shape[1]
    rows = tokens.shape[0] // 2
    full_width = 4 * width
    token_count = tokens.shape[0] * 64
    piece = w_down.shape[0] // 16

    def by_core(own, other):
        return jnp.where(core == 0, own, other), jnp.where(core == 0, other, own)

    up_part = lax.dynamic_slice_in_dim(w_up, group * piece, piece, 1).T
    down_part = lax.dynamic_slice_in_dim(w_down, group * piece, piece, 0)
    both = jnp.stack([tokens.reshape(2, rows, width), target.reshape(2, rows, width)], axis=1)
    own = lax.dynamic_index_in_dim(both, z_half, 0, keepdims=False)
    other = shift_by(lax.dynamic_index_in_dim(both, 1 - z_half, 0, keepdims=False), "zh", 1)
    other, part = lax.optimization_barrier((other, jnp.concatenate([up_part, down_part])))
    joined = jnp.where(
        z_half == 0, jnp.concatenate([own, other], axis=2), jnp.concatenate([other, own], axis=2)
    ).astype(F32)
    values, goal = joined[0], joined[1]

    picked = jnp.where(jnp.arange(plan.shape[0]) == step_index[0], plan, 0)
    time_value = jnp.sum(picked).astype(F32)
    half_width = w_mod.shape[0] // 2
    frequency = jnp.exp(-math.log(10000.0) * jnp.arange(half_width, dtype=F32) / half_width)
    angles = time_value * frequency
    embed = jnp.concatenate([jnp.cos(angles), jnp.sin(angles)])
    level = jax.nn.silu(embed).astype(BF16).astype(F32)[:, None]
    mod = modulate(level, w_mod, core)
    ring, weights = gather_depth(part, place)
    down = jnp.concatenate(
        [jnp.concatenate([weights(4 * h + c)[piece:] for c in range(4)]) for h in (0, 1)], axis=1
    )
    kept, given = split_ring(ring, place, core)
    up = join_cores(kept, shift_by(given, "core", 1), core)
    shift, scale, gate = mod.reshape(3, 2 * width)

    local_mean = jnp.mean(values, axis=1)
    local_dev = jnp.sum(jnp.square(values - local_mean[:, None]), axis=1)
    far_mean, far_dev = shift_by(jnp.stack([local_mean, local_dev]), "core", 1)
    average = 0.5 * (local_mean + far_mean)
    spread = (
        local_dev + far_dev + jnp.square(local_mean - far_mean) * (0.5 * width * 2)
    ) / full_width
    normed = (
        (values - average[:, None]) * lax.rsqrt(spread + 1e-06)[:, None] * (1.0 + scale) + shift
    ).astype(BF16)

    normed_all = gather_plane(normed).reshape(16 * rows, 2 * width)
    hidden = dot(normed_all, up, 1, 1).astype(BF16)
    far = shift_by(hidden, "core", 1)
    activ = activate(hidden, far)
    line = activ.reshape(4, 4 * rows, 4 * piece)
    mixed = {s: dot(line[s], down, 1, 0).astype(BF16) for s in (1, 3, 2, 0)}
    mixed[0], hidden, far = lax.optimization_barrier((mixed[0], hidden, far))
    slope = gelu_slope(hidden, far)
    mixed = sum_line(mixed, True).astype(BF16)
    mixed, slope = lax.optimization_barrier((mixed, slope))
    mixed = sum_line(mixed.reshape(4, rows, 2 * width), False)
    residual = values + gate * mixed - goal
    squares = jnp.broadcast_to(jnp.sum(residual * residual, keepdims=True), (8, 128))
    extra = encode(squares, shift_by(squares, "core", 1), place, width)
    delta = (gate * residual * (1.0 / math.sqrt(token_count))).astype(BF16)

    delta_all = gather_plane(delta).reshape(16 * rows, 2 * width)
    delta_all, extra = lax.optimization_barrier((delta_all, extra))
    hidden_grad = dot(delta_all, down, 1, 1).astype(BF16)
    far = shift_by(hidden_grad, "core", 1)
    down_blocks = [
        dot(activ, delta_all[:, h * width : (h + 1) * width], 0, 0).astype(BF16) for h in (0, 1)
    ]
    down_blocks = jnp.concatenate(down_blocks).reshape(8, piece, width)
    delta_hidden = slope_grad(hidden_grad, far, slope)
    up_grad = jnp.stack(
        [dot(delta_hidden, normed_all[:, h * width : (h + 1) * width], 0, 0).astype(BF16) for h in (0, 1)]
    ).reshape(2, 2, 2, piece, width)
    kept = lax.dynamic_index_in_dim(up_grad, core, 2, keepdims=False)
    given = shift_by(lax.dynamic_index_in_dim(up_grad, 1 - core, 2, keepdims=False), "core", 1)
    pair = by_core(kept, given)
    up_blocks = jnp.stack(pair, axis=2)
    up_blocks = jnp.swapaxes(up_blocks, 0, 1).reshape(8, piece, width)

    grad_down, grad_up = sum_depth(down_blocks, up_blocks, extra, place)
    grad_up = lax.all_to_all(grad_up, PLANE, split_axis=0, concat_axis=0, tiled=True)
    grad_up, loss = unpack(grad_up, 1.0 / (token_count * full_width))
    mean_loss = loss[0, 0]
    return mean_loss, grad_up, grad_down


def solution(mesh):
    fine = Mesh(mesh.devices.reshape([SIZES[name] for name in AXES]), AXES)
    token_spec = P(("y", "x", "zl"), ("zh", "core"))
    weight_spec = P("zl", ("zh", "core"))
    grad_spec = P(("zl", "y", "x"), ("zh", "core"))
    return jax.shard_map(
        per_device,
        mesh=fine,
        in_specs=(token_spec, token_spec, P(PLANE), P(), P(), weight_spec, weight_spec),
        out_specs=(P(), grad_spec, grad_spec),
        check_vma=False,
    )
```
